512 devices in a mesh: tab: 8 (over x_hi, y), rad: 64 (over x_lo, z, core).
Axes of the slice: x: 4 (x_hi: 2, x_lo: 2; x = x_hi * 2 + x_lo), y: 4, z: 16, core: 2. Of those that a mesh axis runs over, the one named last changes fastest.
Arguments:
- poloidal: bfloat16 [1024, 16, 2, 2048], P('rad', None, None, 'tab')
- toroidal: bfloat16 [1024, 16, 2, 2048], P('rad', None, None, 'tab')
- tables: bfloat16 [3, 16, 3072, 2048], P(None, None, 'rad', 'tab'), may hold values from -0.125 to 0.125
- orders: int32 [16], replicated, may hold values from 1 to 127, as said below
Outputs:
- velocity: bfloat16 [3, 8, 3072, 6144], P(None, 'tab', 'rad')
The draws below stay inside these ranges and needn't reach their ends.
Inputs may be any that keep to these rules, and one draw needn't show every extreme that they name: The 16 orders are distinct.
All inputs are finite; a program needn't handle non-finite values.
Results may differ from the reference program's by a relative error of at most 0.02.
Values may be sent and summed in bfloat16 or wider, within the bound.
No kernel may reach another device: no remote copies, remote signals or barrier semaphores. Data moves between devices by JAX's collectives and lax.ppermute only.
A program may use at most 64 MiB of HBM per device.

```python
import math
import jax
import jax.numpy as jnp
from jax import lax

K = 1024
L = 2048
NLAT = 3072
NPHI = 6144
M_WIN = 16
SHELLS = 8


def envelope(exponent, amplitude):
    levels = jnp.arange(K, dtype=jnp.float32)[:, None, None, None]
    degrees = jnp.arange(L, dtype=jnp.float32)[None, None, None, :]
    return amplitude * (levels + 1.0) ** (-exponent) / (degrees + 1.0)


def node_pattern(weights, level_factor, amplitude):
    levels = jnp.arange(K, dtype=jnp.int32)
    degrees = jnp.arange(L, dtype=jnp.float32)[None, None, None, :]
    step_angle = math.pi / (2 * SHELLS)
    pattern = jnp.zeros((K, M_WIN, 2, L), jnp.float32)
    for shell in range(SHELLS):
        turn_counts = levels * (2 * shell + 1) % (4 * SHELLS)
        cosine = jnp.cos(step_angle * turn_counts.astype(jnp.float32))
        pattern = pattern + cosine[:, None, None, None] * weights[shell][None]
    return amplitude / K * level_factor * pattern / (degrees + 1.0)


def draw_poloidal(key, part):
    key = jax.random.fold_in(key, 11)
    normal_key = jax.random.fold_in(key, 0)
    pattern_key = jax.random.fold_in(key, 2)
    level_key = jax.random.fold_in(key, 3)
    draw_shape = (K, M_WIN, 2, L)
    weight_shape = (SHELLS, M_WIN, 2, L)
    level_factor = jnp.exp(jax.random.uniform(level_key, (K, 1, 1, 1), jnp.float32, -0.5, 0.5))
    base_draw = jax.random.normal(normal_key, draw_shape, jnp.float32)
    node_weights = jax.random.normal(pattern_key, weight_shape, jnp.float32)
    combined = envelope(1.5, 0.1) * base_draw + node_pattern(node_weights, level_factor, 0.25)
    return combined.astype(jnp.bfloat16)


def draw_toroidal(key, part):
    key = jax.random.fold_in(key, 23)
    normal_key = jax.random.fold_in(key, 0)
    draw_shape = (K, M_WIN, 2, L)
    base_draw = jax.random.normal(normal_key, draw_shape, jnp.float32)
    return (envelope(0.0, 0.1) * base_draw).astype(jnp.bfloat16)


def draw_orders(key, part):
    key = jax.random.fold_in(key, 5)
    return (jax.random.permutation(key, 127)[:M_WIN] + 1).astype(jnp.int32)


def level_of(rng, shape, shards, low, top_value):
    def one(axis_at, shards_of):
        heights = jax.random.uniform(jax.random.fold_in(jax.random.fold_in(rng, 6), axis_at), (shards_of,), jnp.float32, low / len(shards), top_value / len(shards))
        return jnp.repeat(jnp.exp(heights), shape[axis_at] // shards_of).reshape((-1,) + (1,) * (len(shape) - axis_at - 1))

    gain = one(*shards[0])
    for cut in shards[1:]:
        gain = gain * one(*cut)
    return gain


def bell_draw(key, dims, spread, reach, cuts=(), held_as=jnp.bfloat16):
    result = jax.random.normal(key, dims, jnp.float32) * spread
    if len(cuts) > 0:
        result = level_of(key, dims, cuts, -0.22, 0.18) * result
    return jnp.clip(result, min=-reach, max=reach).astype(held_as)


def setup_inputs(seed: int = 0) -> dict:
    arg_keys = jax.random.split(jax.random.key(seed), 5)
    return {
        "poloidal": draw_poloidal(jax.random.fold_in(arg_keys[4], 71), 0),
        "toroidal": draw_toroidal(jax.random.fold_in(arg_keys[4], 71), 0),
        "tables": bell_draw(arg_keys[2], (3, M_WIN, NLAT, L), L ** -0.5, 0.125, ((2, 64), (3, 8))),
        "orders": draw_orders(jax.random.fold_in(arg_keys[4], 71), 0),
    }


def radial_rows(levels, shell_count):
    odd_numbers = 2 * jnp.arange(shell_count, dtype=jnp.int32) + 1
    turn_counts = levels[None, :] * odd_numbers[:, None] % (4 * shell_count)
    step_angle = math.pi / (2 * shell_count)
    angles = step_angle * turn_counts.astype(jnp.float32)
    node_angle = step_angle * odd_numbers.astype(jnp.float32)
    value_rows = jnp.cos(angles)
    slope_rows = 2.0 * levels.astype(jnp.float32)[None, :] * jnp.sin(angles) / jnp.sin(node_angle)[:, None]
    radius = 1.04 + 0.5 * jnp.cos(node_angle)
    return (value_rows, slope_rows, radius)

def level_terms(value_rows, slope_rows, pol_flat, tor_flat):
    highest = lax.Precision.HIGHEST
    return jnp.stack([jnp.dot(value_rows, pol_flat, precision=highest), jnp.dot(slope_rows, pol_flat, precision=highest), jnp.dot(value_rows, tor_flat, precision=highest)])

def finish(radial, radius, degree_col, order_col):
    degree_wide = degree_col.astype(jnp.float32)
    degree_weight = jnp.where(degree_col >= order_col, jnp.sqrt(degree_wide * (degree_wide + 1.0)), 0.0)
    spheroidal = radial[0] / radius[:, None]
    radial_term = degree_weight * spheroidal
    horizontal_term = degree_weight * (spheroidal + radial[1])
    toroidal_term = degree_weight * radial[2]
    return jnp.stack([radial_term, horizontal_term, toroidal_term]).astype(jnp.bfloat16)

def combine(plain_part, slope_pol, slope_tor, ratio_pol, ratio_tor):
    theta_part = jnp.stack([slope_pol[:, :, 0] - ratio_tor[:, :, 1], slope_pol[:, :, 1] + ratio_tor[:, :, 0]], axis=2)
    phi_part = jnp.stack([-ratio_pol[:, :, 1] - slope_tor[:, :, 0], ratio_pol[:, :, 0] - slope_tor[:, :, 1]], axis=2)
    return jnp.stack([plain_part, theta_part, phi_part])

def longitude_table(orders, points):
    positions = jnp.arange(points, dtype=jnp.int32)
    turn_counts = orders[:, None] * positions[None, :] % points
    angles = 2.0 * math.pi / points * turn_counts.astype(jnp.float32)
    return jnp.concatenate([2.0 * jnp.cos(angles), -2.0 * jnp.sin(angles)], axis=0)

def reference(poloidal, toroidal, tables, orders):
    highest = lax.Precision.HIGHEST
    column_total = M_WIN * 2 * L
    levels = jnp.arange(K, dtype=jnp.int32)
    value_rows, slope_rows, radius = radial_rows(levels, SHELLS)
    pol_flat = poloidal.astype(jnp.float32).reshape(K, column_total)
    tor_flat = toroidal.astype(jnp.float32).reshape(K, column_total)
    radial = level_terms(value_rows, slope_rows, pol_flat, tor_flat)
    column_ids = jnp.arange(column_total, dtype=jnp.int32)
    degree_col = column_ids % L
    order_col = jnp.broadcast_to(orders[:, None, None], (M_WIN, 2, L)).reshape(column_total)
    spectra = finish(radial, radius, degree_col, order_col).reshape(3, SHELLS, M_WIN, 2, L)

    def order_step(order_index):
        table_order = lax.dynamic_index_in_dim(tables, order_index, 1, keepdims=False).astype(jnp.float32)
        coefficients = lax.dynamic_index_in_dim(spectra, order_index, 2, keepdims=False).astype(jnp.float32)

        def project(table_kind, coefficient_kind):
            return jnp.einsum('al,scl->sac', table_order[table_kind], coefficients[coefficient_kind], precision=highest)
        return combine(project(0, 0), project(1, 1), project(1, 2), project(2, 1), project(2, 2))
    fourier = lax.map(order_step, jnp.arange(M_WIN, dtype=jnp.int32))
    fourier = jnp.transpose(fourier, (1, 2, 3, 4, 0)).reshape(3, SHELLS, NLAT, 2 * M_WIN)
    phase_table = longitude_table(orders, NPHI)

    def shell_step(shell_index):
        shell_part = lax.dynamic_index_in_dim(fourier, shell_index, 1, keepdims=False)
        values = jnp.dot(shell_part.reshape(3 * NLAT, 2 * M_WIN), phase_table, precision=highest)
        return values.reshape(3, NLAT, NPHI).astype(jnp.bfloat16)
    velocity = lax.map(shell_step, jnp.arange(SHELLS, dtype=jnp.int32))
    return jnp.moveaxis(velocity, 0, 1)
```

```python
import math

import jax
import jax.numpy as jnp
import numpy as np
from jax import lax
from jax.sharding import Mesh, PartitionSpec as P

NPHI = 6144
SHELLS = 8
RAD = ("xl", "z", "c")
TAB = ("xh", "y")


def radial_rows(levels, shell_count):
    odd_numbers = 2 * jnp.arange(shell_count, dtype=jnp.int32) + 1
    turn_counts = levels[None, :] * odd_numbers[:, None] % (4 * shell_count)
    step_angle = math.pi / (2 * shell_count)
    angles = step_angle * turn_counts.astype(jnp.float32)
    node_angle = step_angle * odd_numbers.astype(jnp.float32)
    value_rows = jnp.cos(angles)
    slope_rows = (
        2.0 * levels.astype(jnp.float32)[None, :] * jnp.sin(angles) / jnp.sin(node_angle)[:, None]
    )
    radius = 1.04 + 0.5 * jnp.cos(node_angle)
    return (value_rows, slope_rows, radius)


def longitude_table(orders, points):
    positions = jnp.arange(points, dtype=jnp.int32)
    turn_counts = orders[:, None] * positions[None, :] % points
    angles = 2.0 * math.pi / points * turn_counts.astype(jnp.float32)
    return jnp.concatenate([2.0 * jnp.cos(angles), -2.0 * jnp.sin(angles)], axis=0)


def split_bf16(x):
    hi = lax.reduce_precision(x, 8, 7)
    return hi.astype(jnp.bfloat16), (x - hi).astype(jnp.bfloat16)


def dot32(a, b):
    return jnp.dot(a, b, preferred_element_type=jnp.float32)


def on_device(poloidal, toroidal, tables, orders):
    xl, z, c = (lax.axis_index(n) for n in RAD)
    tab = lax.axis_index(TAB)
    level_dev, order_count, _, degree_dev = poloidal.shape
    half = order_count // 2
    blocks = half * 2 * degree_dev // 128
    rad_pair = xl * 16 + z
    pol = lax.all_gather(poloidal, "c", axis=0, tiled=True)
    tor = lax.all_gather(toroidal, "c", axis=0, tiled=True)
    pol = lax.dynamic_slice_in_dim(pol, c * half, half, 1).reshape(2 * level_dev, -1)
    tor = lax.dynamic_slice_in_dim(tor, c * half, half, 1).reshape(2 * level_dev, -1)
    levels = rad_pair * 2 * level_dev + jnp.arange(2 * level_dev, dtype=jnp.int32)
    value_rows, slope_rows, radius = radial_rows(levels, SHELLS)
    pol_hi, pol_lo = split_bf16(jnp.concatenate([value_rows, slope_rows]))
    tor_hi, tor_lo = pol_hi[:SHELLS], pol_lo[:SHELLS]
    partial = jnp.concatenate(
        [
            dot32(pol_hi, pol) + dot32(pol_lo, pol),
            dot32(tor_hi, tor) + dot32(tor_lo, tor),
        ]
    ).astype(jnp.bfloat16)
    partial = partial.reshape(3 * SHELLS, blocks, 128).transpose(1, 0, 2)
    shares = lax.all_to_all(partial, ("xl", "z"), 0, 0, tiled=True)
    radial = jnp.sum(shares.astype(jnp.float32), axis=0).reshape(3, SHELLS, 128)

    order = orders[c * half + rad_pair // 4]
    degree = tab * degree_dev + (rad_pair % 2) * 128 + jnp.arange(128, dtype=jnp.int32)
    degree_wide = degree.astype(jnp.float32)
    weight = jnp.where(degree >= order, jnp.sqrt(degree_wide * (degree_wide + 1.0)), 0.0)
    spheroidal = radial[0] / radius[:, None]
    spectra = jnp.stack(
        [weight * spheroidal, weight * (spheroidal + radial[1]), weight * radial[2]]
    ).astype(jnp.bfloat16)
    spectra = jnp.broadcast_to(spectra.reshape(1, 3 * SHELLS, 128), (blocks, 3 * SHELLS, 128))
    spectra = lax.all_to_all(spectra, ("xl", "z"), 0, 0, tiled=True)
    spectra = lax.all_gather(spectra, "c", axis=0, tiled=True)
    coef = spectra.reshape(order_count, 2, 2, 3, SHELLS, 128).transpose(3, 0, 4, 1, 2, 5)
    coef = coef.reshape(3, order_count, SHELLS, 2, degree_dev)

    q, s, t = coef[0], coef[1], coef[2]
    swap = lambda v: jnp.stack([-v[:, :, 1], v[:, :, 0]], axis=2)
    theta = jnp.concatenate([s, swap(t)], axis=-1)
    phi = jnp.concatenate([-t, swap(s)], axis=-1)
    both = jnp.concatenate([theta, phi], axis=1)
    pair_table = jnp.concatenate([tables[1], tables[2]], axis=-1)
    plain = jnp.einsum("mscl,mal->mcsa", q, tables[0], preferred_element_type=jnp.float32)
    pair = jnp.einsum("mscl,mal->mcsa", both, pair_table, preferred_element_type=jnp.float32)
    fourier = jnp.stack([plain, pair[:, :, :SHELLS], pair[:, :, SHELLS:]])
    fourier = fourier.transpose(3, 2, 1, 0, 4).reshape(SHELLS, 2 * order_count, -1)
    fourier = lax.all_to_all(fourier.astype(jnp.bfloat16), TAB, 0, 0, tiled=True)
    summed = jnp.sum(fourier.astype(jnp.float32), axis=0)
    f_hi, f_lo = split_bf16(summed)
    p_hi, p_lo = split_bf16(longitude_table(orders, NPHI))
    values = lax.dot_general(
        jnp.concatenate([f_hi, f_hi, f_lo]),
        jnp.concatenate([p_hi, p_lo, p_hi]),
        (((0,), (0,)), ((), ())),
        preferred_element_type=jnp.float32,
    )
    return values.astype(jnp.bfloat16).reshape(3, 1, -1, NPHI)


def solution(mesh):
    fine = Mesh(mesh.devices.reshape(2, 4, 2, 16, 2), TAB + RAD)
    placed = (
        P(RAD, None, None, TAB),
        P(RAD, None, None, TAB),
        P(None, None, RAD, TAB),
        P(),
    )
    return jax.shard_map(
        on_device,
        mesh=fine,
        in_specs=placed,
        out_specs=P(None, TAB, RAD, None),
        check_vma=False,
    )
```

```python
import math

import jax
import jax.numpy as jnp
from jax import lax
from jax.experimental import pallas as pl
from jax.experimental.pallas import tpu as pltpu
from jax.sharding import Mesh, PartitionSpec as P

NPHI = 6144
SHELLS = 8
RAD = ("xl", "z", "c")
TAB = ("xh", "y")


def shell_radius():
    return 1.04 + 0.5 * jnp.cos(math.pi / (2 * SHELLS) * (2 * jnp.arange(SHELLS) + 1))


def level_matrix(first_level, level_dev):
    shape = (2 * 3 * SHELLS, 4 * level_dev * 2)
    row = lax.broadcasted_iota(jnp.int32, shape, 0)
    col = lax.broadcasted_iota(jnp.int32, shape, 1)
    kind = row % (3 * SHELLS) // SHELLS
    odd = 2 * (row % SHELLS) + 1
    level = first_level + col % (2 * level_dev) // 2
    source = col // (2 * level_dev)
    step_angle = math.pi / (2 * SHELLS)
    angle = step_angle * (level * odd % (4 * SHELLS)).astype(jnp.float32)
    node_angle = step_angle * odd.astype(jnp.float32)
    slope = 2.0 * level.astype(jnp.float32) * jnp.sin(angle) / jnp.sin(node_angle)
    entry = jnp.where(kind == 1, slope, jnp.cos(angle))
    high = lax.reduce_precision(entry, 8, 7)
    entry = jnp.where(source % 2 == 0, high, entry - high)
    used = (row // (3 * SHELLS) == col % 2) & ((kind < 2) == (source < 2))
    return jnp.where(used, entry, 0.0).astype(jnp.bfloat16)


def level_kernel(matrix_ref, pol_ref, tor_ref, out_ref):
    level_dev, order_count, _, degree_dev = pol_ref.shape
    rows = out_ref.shape[1]
    matrix = matrix_ref[...]
    for order in range(order_count):
        pol = pol_ref[:, order].reshape(2 * level_dev, degree_dev)
        tor = tor_ref[:, order].reshape(2 * level_dev, degree_dev)
        sums = dot32(matrix, jnp.concatenate([pol, pol, tor, tor], axis=0))
        for part in range(2):
            for cut in range(degree_dev // 128):
                block = sums[part * rows : (part + 1) * rows, cut * 128 : (cut + 1) * 128]
                out_ref[(order * 2 + part) * (degree_dev // 128) + cut] = block.astype(jnp.bfloat16)


def level_sums(matrix, poloidal, toroidal):
    _, order_count, _, degree_dev = poloidal.shape
    return pl.pallas_call(
        level_kernel,
        out_shape=jax.ShapeDtypeStruct(
            (order_count * 2 * degree_dev // 128, 3 * SHELLS, 128), jnp.bfloat16
        ),
        compiler_params=pltpu.CompilerParams(vmem_limit_bytes=60 << 20),
        name="level_sums",
    )(matrix, poloidal, toroidal)


def longitude_table(orders, points):
    positions = jnp.arange(points, dtype=jnp.int32)
    turn_counts = orders[:, None] * positions[None, :] % points
    angles = 2.0 * math.pi / points * turn_counts.astype(jnp.float32)
    return jnp.concatenate([2.0 * jnp.cos(angles), -2.0 * jnp.sin(angles)], axis=0)


def split_bf16(x):
    hi = lax.reduce_precision(x, 8, 7)
    return hi.astype(jnp.bfloat16), (x - hi).astype(jnp.bfloat16)


def dot32(a, b):
    return jnp.dot(a, b, preferred_element_type=jnp.float32)


def on_device(poloidal, toroidal, tables, orders):
    xl, z, c = (lax.axis_index(n) for n in RAD)
    tab = lax.axis_index(TAB)
    level_dev, order_count, _, degree_dev = poloidal.shape
    half = order_count // 2
    blocks = half * 2 * degree_dev // 128
    rad_pair = xl * 16 + z
    matrix = level_matrix((rad_pair * 2 + c) * level_dev, level_dev)
    partial = level_sums(matrix, poloidal, toroidal)
    pair = lax.all_gather(partial, "c", axis=0)
    pair = lax.dynamic_slice_in_dim(pair, c * blocks, blocks, 1).astype(jnp.float32)
    partial = (pair[0] + pair[1]).astype(jnp.bfloat16)
    shares = lax.all_to_all(partial, ("xl", "z"), 0, 0, tiled=True)
    radial = jnp.sum(shares.astype(jnp.float32), axis=0).reshape(3, SHELLS, 128)

    order = orders[c * half + rad_pair // 4]
    degree = tab * degree_dev + (rad_pair % 2) * 128 + jnp.arange(128, dtype=jnp.int32)
    degree_wide = degree.astype(jnp.float32)
    weight = jnp.where(degree >= order, jnp.sqrt(degree_wide * (degree_wide + 1.0)), 0.0)
    spheroidal = radial[0] / shell_radius()[:, None]
    spectra = jnp.stack(
        [weight * spheroidal, weight * (spheroidal + radial[1]), weight * radial[2]]
    ).astype(jnp.bfloat16)
    spectra = jnp.broadcast_to(spectra.reshape(1, 3 * SHELLS, 128), (blocks, 3 * SHELLS, 128))
    spectra = lax.all_to_all(spectra, ("xl", "z"), 0, 0, tiled=True)
    spectra = lax.all_gather(spectra, "c", axis=0, tiled=True)
    coef = spectra.reshape(order_count, 2, 2, 3, SHELLS, 128).transpose(3, 0, 4, 1, 2, 5)
    coef = coef.reshape(3, order_count, SHELLS, 2, degree_dev)

    q, s, t = coef[0], coef[1], coef[2]
    swap = lambda v: jnp.stack([-v[:, :, 1], v[:, :, 0]], axis=2)
    theta = jnp.concatenate([s, swap(t)], axis=-1)
    phi = jnp.concatenate([-t, swap(s)], axis=-1)
    both = jnp.concatenate([theta, phi], axis=1)
    pair_table = jnp.concatenate([tables[1], tables[2]], axis=-1)
    plain = jnp.einsum("mscl,mal->mcsa", q, tables[0], preferred_element_type=jnp.float32)
    pair = jnp.einsum("mscl,mal->mcsa", both, pair_table, preferred_element_type=jnp.float32)
    fourier = jnp.stack([plain, pair[:, :, :SHELLS], pair[:, :, SHELLS:]])
    fourier = fourier.transpose(3, 2, 1, 0, 4).reshape(SHELLS, 2 * order_count, -1)
    fourier = lax.all_to_all(fourier.astype(jnp.bfloat16), TAB, 0, 0, tiled=True)
    summed = jnp.sum(fourier.astype(jnp.float32), axis=0)
    f_hi, f_lo = split_bf16(summed)
    p_hi, p_lo = split_bf16(longitude_table(orders, NPHI))
    values = lax.dot_general(
        jnp.concatenate([f_hi, f_hi, f_lo]),
        jnp.concatenate([p_hi, p_lo, p_hi]),
        (((0,), (0,)), ((), ())),
        preferred_element_type=jnp.float32,
    )
    return values.astype(jnp.bfloat16).reshape(3, 1, -1, NPHI)


def solution(mesh):
    fine = Mesh(mesh.devices.reshape(2, 4, 2, 16, 2), TAB + RAD)
    placed = (
        P(RAD, None, None, TAB),
        P(RAD, None, None, TAB),
        P(None, None, RAD, TAB),
        P(),
    )
    return jax.shard_map(
        on_device,
        mesh=fine,
        in_specs=placed,
        out_specs=P(None, TAB, RAD, None),
        check_vma=False,
    )
```

```python
import math

import jax
import jax.numpy as jnp
from jax import lax
from jax.experimental import pallas as pl
from jax.experimental.pallas import tpu as pltpu
from jax.sharding import Mesh, PartitionSpec as P

NPHI = 6144
SHELLS = 8
RAD = ("xl", "zf", "zn", "c")
NEAR = ("xl", "zn")
TAB = ("xh", "y")


def shell_radius():
    return 1.04 + 0.5 * jnp.cos(math.pi / (2 * SHELLS) * (2 * jnp.arange(SHELLS) + 1))


def level_matrix(first_level, level_dev):
    shape = (2 * 3 * SHELLS, 4 * level_dev * 2)
    row = lax.broadcasted_iota(jnp.int32, shape, 0)
    col = lax.broadcasted_iota(jnp.int32, shape, 1)
    kind = row % (3 * SHELLS) // SHELLS
    odd = 2 * (row % SHELLS) + 1
    level = first_level + col % (2 * level_dev) // 2
    source = col // (2 * level_dev)
    step_angle = math.pi / (2 * SHELLS)
    angle = step_angle * (level * odd % (4 * SHELLS)).astype(jnp.float32)
    node_angle = step_angle * odd.astype(jnp.float32)
    slope = 2.0 * level.astype(jnp.float32) * jnp.sin(angle) / jnp.sin(node_angle)
    entry = jnp.where(kind == 1, slope, jnp.cos(angle))
    high = lax.reduce_precision(entry, 8, 7)
    entry = jnp.where(source % 2 == 0, high, entry - high)
    used = (row // (3 * SHELLS) == col % 2) & ((kind < 2) == (source < 2))
    return jnp.where(used, entry, 0.0).astype(jnp.bfloat16)


def level_kernel(matrix_ref, pol_ref, tor_ref, out_ref):
    level_dev, order_count, _, degree_dev = pol_ref.shape
    rows = out_ref.shape[1]
    matrix = matrix_ref[...]
    for order in range(order_count):
        pol = pol_ref[:, order].reshape(2 * level_dev, degree_dev)
        tor = tor_ref[:, order].reshape(2 * level_dev, degree_dev)
        sums = dot32(matrix, jnp.concatenate([pol, pol, tor, tor], axis=0))
        for part in range(2):
            for cut in range(degree_dev // 128):
                block = sums[part * rows : (part + 1) * rows, cut * 128 : (cut + 1) * 128]
                out_ref[(order * 2 + part) * (degree_dev // 128) + cut] = block.astype(jnp.bfloat16)


def level_sums(matrix, poloidal, toroidal):
    _, order_count, _, degree_dev = poloidal.shape
    return pl.pallas_call(
        level_kernel,
        out_shape=jax.ShapeDtypeStruct(
            (order_count * 2 * degree_dev // 128, 3 * SHELLS, 128), jnp.bfloat16
        ),
        compiler_params=pltpu.CompilerParams(vmem_limit_bytes=60 << 20),
        name="level_sums",
    )(matrix, poloidal, toroidal)


def longitude_table(orders, points):
    positions = jnp.arange(points, dtype=jnp.int32)
    turn_counts = orders[:, None] * positions[None, :] % points
    angles = 2.0 * math.pi / points * turn_counts.astype(jnp.float32)
    return jnp.concatenate([2.0 * jnp.cos(angles), -2.0 * jnp.sin(angles)], axis=0)


def split_bf16(x):
    hi = lax.reduce_precision(x, 8, 7)
    return hi.astype(jnp.bfloat16), (x - hi).astype(jnp.bfloat16)


def dot32(a, b):
    return jnp.dot(a, b, preferred_element_type=jnp.float32)


def on_device(poloidal, toroidal, tables, orders):
    c = lax.axis_index("c")
    tab = lax.axis_index(TAB)
    level_dev, order_count, _, degree_dev = poloidal.shape
    half = order_count // 2
    blocks = half * 2 * degree_dev // 128
    near = lax.axis_index(NEAR)
    near_count = lax.axis_size(NEAR)
    far_count = lax.axis_size("zf")
    matrix = level_matrix(lax.axis_index(RAD) * level_dev, level_dev)
    partial = level_sums(matrix, poloidal, toroidal)
    pair = lax.all_gather(partial, "c", axis=0)
    pair = lax.dynamic_slice_in_dim(pair, c * blocks, blocks, 1).astype(jnp.float32)
    partial = (pair[0] + pair[1]).astype(jnp.bfloat16)
    shares = lax.all_to_all(partial, NEAR, 0, 0, tiled=True)
    shares = shares.reshape(near_count, -1, 3 * SHELLS, 128).astype(jnp.float32)
    copies = jnp.broadcast_to(
        jnp.sum(shares, axis=0).astype(jnp.bfloat16), (far_count,) + shares.shape[1:]
    )
    shares = lax.all_to_all(copies, "zf", 0, 0, tiled=True)
    radial = jnp.sum(shares.astype(jnp.float32), axis=0)
    radial = radial.reshape(2, degree_dev // 128, 3, SHELLS, 128)

    order = lax.dynamic_index_in_dim(orders, c * half + near, keepdims=False)
    degree = tab * degree_dev + jnp.arange(degree_dev, dtype=jnp.int32)
    degree_wide = degree.astype(jnp.float32)
    weight = jnp.where(degree >= order, jnp.sqrt(degree_wide * (degree_wide + 1.0)), 0.0)
    weight = weight.reshape(1, degree_dev // 128, 1, 128)
    spheroidal = radial[:, :, 0] / shell_radius()[:, None]
    spectra = jnp.stack(
        [
            weight * spheroidal,
            weight * (spheroidal + radial[:, :, 1]),
            weight * radial[:, :, 2],
        ],
        axis=2,
    ).astype(jnp.bfloat16)
    spectra = jnp.broadcast_to(
        spectra.reshape(1, -1, 3 * SHELLS, 128), (near_count, blocks // near_count, 3 * SHELLS, 128)
    )
    spectra = lax.all_to_all(spectra, NEAR, 0, 0, tiled=True)
    spectra = lax.all_gather(spectra, "c", axis=0, tiled=True)
    coef = spectra.reshape(order_count, 2, 2, 3, SHELLS, 128).transpose(3, 0, 4, 1, 2, 5)
    coef = coef.reshape(3, order_count, SHELLS, 2, degree_dev)

    q, s, t = coef[0], coef[1], coef[2]
    swap = lambda v: jnp.stack([-v[:, :, 1], v[:, :, 0]], axis=2)
    theta = jnp.concatenate([s, swap(t)], axis=-1)
    phi = jnp.concatenate([-t, swap(s)], axis=-1)
    both = jnp.concatenate([theta, phi], axis=1)
    pair_table = jnp.concatenate([tables[1], tables[2]], axis=-1)
    plain = jnp.einsum("mscl,mal->mcsa", q, tables[0], preferred_element_type=jnp.float32)
    pair = jnp.einsum("mscl,mal->mcsa", both, pair_table, preferred_element_type=jnp.float32)
    fourier = jnp.stack([plain, pair[:, :, :SHELLS], pair[:, :, SHELLS:]])
    fourier = fourier.transpose(3, 2, 1, 0, 4).reshape(SHELLS, 2 * order_count, -1)
    fourier = lax.all_to_all(fourier.astype(jnp.bfloat16), TAB, 0, 0, tiled=True)
    summed = jnp.sum(fourier.astype(jnp.float32), axis=0)
    f_hi, f_lo = split_bf16(summed)
    p_hi, p_lo = split_bf16(longitude_table(orders, NPHI))
    values = lax.dot_general(
        jnp.concatenate([f_hi, f_hi, f_lo]),
        jnp.concatenate([p_hi, p_lo, p_hi]),
        (((0,), (0,)), ((), ())),
        preferred_element_type=jnp.float32,
    )
    return values.astype(jnp.bfloat16).reshape(3, 1, -1, NPHI)


def solution(mesh):
    fine = Mesh(mesh.devices.reshape(2, 4, 2, 4, 4, 2), TAB + RAD)
    placed = (
        P(RAD, None, None, TAB),
        P(RAD, None, None, TAB),
        P(None, None, RAD, TAB),
        P(),
    )
    return jax.shard_map(
        on_device,
        mesh=fine,
        in_specs=placed,
        out_specs=P(None, TAB, RAD, None),
        check_vma=False,
    )
```

```python
import math

import jax
import jax.numpy as jnp
import numpy as np
from jax import lax
from jax.experimental import pallas as pl
from jax.experimental.pallas import tpu as pltpu
from jax.sharding import Mesh, PartitionSpec as P

NPHI = 6144
SHELLS = 8
RAD = ("xl", "zf", "zn", "c")
NEAR = ("xl", "zn")
TAB = ("xh", "y")


def shell_radius():
    angle = math.pi / (2 * SHELLS) * (2 * np.arange(SHELLS) + 1)
    return (1.04 + 0.5 * np.cos(angle)).astype(np.float32)


def level_constants(level_dev):
    row = np.arange(2 * 3 * SHELLS)[:, None]
    col = np.arange(4 * level_dev * 2)[None, :]
    kind = row % (3 * SHELLS) // SHELLS
    odd = 2 * (row % SHELLS) + 1
    source = col // (2 * level_dev)
    used = (row // (3 * SHELLS) == col % 2) & ((kind < 2) == (source < 2))
    step_angle = math.pi / (2 * SHELLS)
    planes = []
    for parity in range(4 * SHELLS // level_dev):
        level = parity * level_dev + col % (2 * level_dev) // 2
        angle = step_angle * (level * odd % (4 * SHELLS))
        value = np.where(used & (kind != 1), np.cos(angle), 0.0)
        slope = np.where(used & (kind == 1), 2.0 * np.sin(angle) / np.sin(step_angle * odd), 0.0)
        planes.append(np.stack([value, slope]))
    return np.stack(planes).astype(np.float32)


def level_kernel(constant_ref, pol_ref, tor_ref, out_ref):
    level_dev, order_count, _, degree_dev = pol_ref.shape
    rows = out_ref.shape[1]
    run = lax.axis_index(RAD)
    plane = lax.rem(run, constant_ref.shape[0])
    col = lax.broadcasted_iota(jnp.int32, constant_ref.shape[2:], 1)
    level = (run * level_dev + col % (2 * level_dev) // 2).astype(jnp.float32)
    entry = constant_ref[plane, 0] + level * constant_ref[plane, 1]
    high = entry.astype(jnp.bfloat16)
    low = (entry - high.astype(jnp.float32)).astype(jnp.bfloat16)
    matrix = jnp.where(col // (2 * level_dev) % 2 == 0, high, low)
    for order in range(order_count):
        pol = pol_ref[:, order].reshape(2 * level_dev, degree_dev)
        tor = tor_ref[:, order].reshape(2 * level_dev, degree_dev)
        sums = dot32(matrix, jnp.concatenate([pol, pol, tor, tor], axis=0))
        for part in range(2):
            for cut in range(degree_dev // 128):
                block = sums[part * rows : (part + 1) * rows, cut * 128 : (cut + 1) * 128]
                out_ref[(order * 2 + part) * (degree_dev // 128) + cut] = block.astype(jnp.bfloat16)


def level_sums(poloidal, toroidal):
    level_dev, order_count, _, degree_dev = poloidal.shape
    return pl.pallas_call(
        level_kernel,
        out_shape=jax.ShapeDtypeStruct(
            (order_count * 2 * degree_dev // 128, 3 * SHELLS, 128), jnp.bfloat16
        ),
        compiler_params=pltpu.CompilerParams(vmem_limit_bytes=60 << 20),
        name="level_sums",
    )(level_constants(level_dev), poloidal, toroidal)


def longitude_table(orders, points):
    positions = jnp.arange(points, dtype=jnp.int32)
    turn_counts = orders[:, None] * positions[None, :] % points
    angles = 2.0 * math.pi / points * turn_counts.astype(jnp.float32)
    return jnp.concatenate([2.0 * jnp.cos(angles), -2.0 * jnp.sin(angles)], axis=0)


def split_bf16(x):
    hi = lax.reduce_precision(x, 8, 7)
    return hi.astype(jnp.bfloat16), (x - hi).astype(jnp.bfloat16)


def dot32(a, b):
    return jnp.dot(a, b, preferred_element_type=jnp.float32)


def on_device(poloidal, toroidal, tables, orders):
    c = lax.axis_index("c")
    tab = lax.axis_index(TAB)
    _, order_count, _, degree_dev = poloidal.shape
    half = order_count // 2
    blocks = half * 2 * degree_dev // 128
    near = lax.axis_index(NEAR)
    near_count = lax.axis_size(NEAR)
    far_count = lax.axis_size("zf")
    own_order = c * half + near
    first_degree = tab * degree_dev
    first_block = c * blocks
    partial = level_sums(poloidal, toroidal)
    partial, own_order, first_degree, first_block = lax.optimization_barrier(
        (partial, own_order, first_degree, first_block)
    )
    pair = lax.all_gather(partial, "c", axis=0)
    pair = lax.dynamic_slice_in_dim(pair, first_block, blocks, 1).astype(jnp.float32)
    partial = (pair[0] + pair[1]).astype(jnp.bfloat16)
    shares = lax.all_to_all(partial, NEAR, 0, 0, tiled=True)
    shares = shares.reshape(near_count, -1, 3 * SHELLS, 128).astype(jnp.float32)
    near_sum = lax.optimization_barrier(jnp.sum(shares, axis=0))
    copies = jnp.broadcast_to(near_sum.astype(jnp.bfloat16), (far_count,) + near_sum.shape)
    copies, orders, tables = lax.optimization_barrier((copies, orders, tables))
    shares = lax.all_to_all(copies, "zf", 0, 0, tiled=True)
    order = jnp.sum(jnp.where(jnp.arange(order_count) == own_order, orders, 0))
    degree = first_degree + jnp.arange(degree_dev, dtype=jnp.int32)
    degree_wide = degree.astype(jnp.float32)
    weight = jnp.where(degree >= order, jnp.sqrt(degree_wide * (degree_wide + 1.0)), 0.0)
    weight = weight.reshape(1, degree_dev // 128, 1, 128)
    p_hi, p_lo = split_bf16(longitude_table(orders, NPHI))
    pair_table = jnp.concatenate([tables[1], tables[2]], axis=-1)
    shares, weight, p_hi, p_lo, plain_table, pair_table = lax.optimization_barrier(
        (shares, weight, p_hi, p_lo, tables[0], pair_table)
    )
    radial = jnp.sum(shares.astype(jnp.float32), axis=0)
    radial = radial.reshape(2, degree_dev // 128, 3, SHELLS, 128)
    spheroidal = radial[:, :, 0] / shell_radius()[:, None]
    spectra = jnp.stack(
        [
            weight * spheroidal,
            weight * (spheroidal + radial[:, :, 1]),
            weight * radial[:, :, 2],
        ],
        axis=2,
    ).astype(jnp.bfloat16)
    spectra = jnp.broadcast_to(
        spectra.reshape(1, -1, 3 * SHELLS, 128), (near_count, blocks // near_count, 3 * SHELLS, 128)
    )
    spectra = lax.all_to_all(spectra, NEAR, 0, 0, tiled=True)
    spectra = lax.all_gather(spectra, "c", axis=0, tiled=True)
    coef = spectra.reshape(order_count, 2, 2, 3, SHELLS, 128).transpose(3, 0, 4, 1, 2, 5)
    coef = coef.reshape(3, order_count, SHELLS, 2, degree_dev)

    q, s, t = coef[0], coef[1], coef[2]
    swap = lambda v: jnp.stack([-v[:, :, 1], v[:, :, 0]], axis=2)
    theta = jnp.concatenate([s, swap(t)], axis=-1)
    phi = jnp.concatenate([-t, swap(s)], axis=-1)
    both = jnp.concatenate([theta, phi], axis=1)
    plain = jnp.einsum("mscl,mal->mcsa", q, plain_table, preferred_element_type=jnp.float32)
    pair = jnp.einsum("mscl,mal->mcsa", both, pair_table, preferred_element_type=jnp.float32)
    fourier = jnp.stack([plain, pair[:, :, :SHELLS], pair[:, :, SHELLS:]])
    fourier = fourier.transpose(3, 2, 1, 0, 4).reshape(SHELLS, 2 * order_count, -1)
    fourier = lax.all_to_all(fourier.astype(jnp.bfloat16), TAB, 0, 0, tiled=True)
    summed = jnp.sum(fourier.astype(jnp.float32), axis=0)
    f_hi, f_lo = split_bf16(summed)
    values = lax.dot_general(
        jnp.concatenate([f_hi, f_hi, f_lo]),
        jnp.concatenate([p_hi, p_lo, p_hi]),
        (((0,), (0,)), ((), ())),
        preferred_element_type=jnp.float32,
    )
    return values.astype(jnp.bfloat16).reshape(3, 1, -1, NPHI)


def solution(mesh):
    fine = Mesh(mesh.devices.reshape(2, 4, 2, 4, 4, 2), TAB + RAD)
    placed = (
        P(RAD, None, None, TAB),
        P(RAD, None, None, TAB),
        P(None, None, RAD, TAB),
        P(),
    )
    return jax.shard_map(
        on_device,
        mesh=fine,
        in_specs=placed,
        out_specs=P(None, TAB, RAD, None),
        check_vma=False,
    )
```

```python
import math

import jax
import jax.numpy as jnp
import numpy as np
from jax import lax
from jax.experimental import pallas as pl
from jax.experimental.pallas import tpu as pltpu
from jax.sharding import Mesh, PartitionSpec as P

NPHI = 6144
SHELLS = 8
RAD = ("xl", "zf", "zn", "c")
NEAR = ("xl", "zn")
NEAR_ORDER = (5, 6, 7, 4, 1, 2, 3, 0)
FAR_ORDER = (2, 3, 0, 1)
TAB_ORDER = (7, 6, 5, 4, 3, 2, 1, 0)
TAB = ("xh", "y")


def shell_radius():
    angle = math.pi / (2 * SHELLS) * (2 * np.array(TAB_ORDER) + 1)
    return (1.04 + 0.5 * np.cos(angle)).astype(np.float32)


def level_constants(level_dev):
    row = np.arange(2 * 3 * SHELLS)[:, None]
    col = np.arange(4 * level_dev * 2)[None, :]
    kind = row % (3 * SHELLS) // SHELLS
    odd = 2 * np.array(TAB_ORDER)[row % SHELLS] + 1
    source = col // (2 * level_dev)
    used = (row // (3 * SHELLS) == col % 2) & ((kind < 2) == (source < 2))
    step_angle = math.pi / (2 * SHELLS)
    planes = []
    for parity in range(4 * SHELLS // level_dev):
        level = parity * level_dev + col % (2 * level_dev) // 2
        angle = step_angle * (level * odd % (4 * SHELLS))
        value = np.where(used & (kind != 1), np.cos(angle), 0.0)
        slope = np.where(used & (kind == 1), 2.0 * np.sin(angle) / np.sin(step_angle * odd), 0.0)
        planes.append(np.stack([value, slope]))
    return np.stack(planes).astype(np.float32)


def level_kernel(constant_ref, pol_ref, tor_ref, out_ref):
    level_dev, order_count, _, degree_dev = pol_ref.shape
    rows = out_ref.shape[1]
    run = lax.axis_index(RAD)
    plane = lax.rem(run, constant_ref.shape[0])
    col = lax.broadcasted_iota(jnp.int32, constant_ref.shape[2:], 1)
    level = (run * level_dev + col % (2 * level_dev) // 2).astype(jnp.float32)
    entry = constant_ref[plane, 0] + level * constant_ref[plane, 1]
    high = entry.astype(jnp.bfloat16)
    low = (entry - high.astype(jnp.float32)).astype(jnp.bfloat16)
    matrix = jnp.where(col // (2 * level_dev) % 2 == 0, high, low)
    for order in range(order_count):
        pol = pol_ref[:, order].reshape(2 * level_dev, degree_dev)
        tor = tor_ref[:, order].reshape(2 * level_dev, degree_dev)
        sums = dot32(matrix, jnp.concatenate([pol, pol, tor, tor], axis=0))
        for part in range(2):
            for cut in range(degree_dev // 128):
                block = sums[part * rows : (part + 1) * rows, cut * 128 : (cut + 1) * 128]
                out_ref[(order * 2 + part) * (degree_dev // 128) + cut] = block.astype(jnp.bfloat16)


def level_sums(poloidal, toroidal):
    level_dev, order_count, _, degree_dev = poloidal.shape
    return pl.pallas_call(
        level_kernel,
        out_shape=jax.ShapeDtypeStruct(
            (order_count * 2 * degree_dev // 128, 3 * SHELLS, 128), jnp.bfloat16
        ),
        compiler_params=pltpu.CompilerParams(vmem_limit_bytes=60 << 20),
        name="level_sums",
    )(level_constants(level_dev), poloidal, toroidal)


def longitude_table(orders, points):
    positions = jnp.arange(points, dtype=jnp.int32)
    turn_counts = orders[:, None] * positions[None, :] % points
    angles = 2.0 * math.pi / points * turn_counts.astype(jnp.float32)
    return jnp.concatenate([2.0 * jnp.cos(angles), -2.0 * jnp.sin(angles)], axis=0)


def split_bf16(x):
    hi = lax.reduce_precision(x, 8, 7)
    return hi.astype(jnp.bfloat16), (x - hi).astype(jnp.bfloat16)


def dot32(a, b):
    return jnp.dot(a, b, preferred_element_type=jnp.float32)


def on_device(poloidal, toroidal, tables, orders):
    c = lax.axis_index("c")
    tab = lax.axis_index(TAB)
    _, order_count, _, degree_dev = poloidal.shape
    half = order_count // 2
    blocks = half * 2 * degree_dev // 128
    near = (1 - lax.axis_index("xl")) * 4 + (lax.axis_index("zn") + 3) % 4
    near_count = lax.axis_size(NEAR)
    far_count = lax.axis_size("zf")
    own_order = c * half + near
    first_degree = tab * degree_dev
    first_block = c * blocks
    partial = level_sums(poloidal, toroidal)
    partial, own_order, first_degree, first_block = lax.optimization_barrier(
        (partial, own_order, first_degree, first_block)
    )
    pair = lax.all_gather(partial, "c", axis=0)
    pair = lax.dynamic_slice_in_dim(pair, first_block, blocks, 1).astype(jnp.float32)
    partial = (pair[0] + pair[1]).astype(jnp.bfloat16)
    shares = lax.all_to_all(partial, NEAR, 0, 0, axis_index_groups=[NEAR_ORDER], tiled=True)
    shares = shares.reshape(near_count, -1, 3 * SHELLS, 128).astype(jnp.float32)
    near_sum = lax.optimization_barrier(jnp.sum(shares, axis=0))
    copies = jnp.broadcast_to(near_sum.astype(jnp.bfloat16), (far_count,) + near_sum.shape)
    copies, orders, tables = lax.optimization_barrier((copies, orders, tables))
    shares = lax.all_to_all(copies, "zf", 0, 0, axis_index_groups=[FAR_ORDER], tiled=True)
    order = jnp.sum(jnp.where(jnp.arange(order_count) == own_order, orders, 0))
    degree = first_degree + jnp.arange(degree_dev, dtype=jnp.int32)
    degree_wide = degree.astype(jnp.float32)
    weight = jnp.where(degree >= order, jnp.sqrt(degree_wide * (degree_wide + 1.0)), 0.0)
    weight = weight.reshape(1, degree_dev // 128, 1, 128)
    p_hi, p_lo = split_bf16(longitude_table(orders, NPHI))
    pair_table = jnp.concatenate([tables[1], tables[2]], axis=-1)
    shares, weight, p_hi, p_lo, plain_table, pair_table = lax.optimization_barrier(
        (shares, weight, p_hi, p_lo, tables[0], pair_table)
    )
    radial = jnp.sum(shares.astype(jnp.float32), axis=0)
    radial = radial.reshape(2, degree_dev // 128, 3, SHELLS, 128)
    spheroidal = radial[:, :, 0] / shell_radius()[:, None]
    spectra = jnp.stack(
        [
            weight * spheroidal,
            weight * (spheroidal + radial[:, :, 1]),
            weight * radial[:, :, 2],
        ],
        axis=2,
    ).astype(jnp.bfloat16)
    spectra = jnp.broadcast_to(
        spectra.reshape(1, -1, 3 * SHELLS, 128), (near_count, blocks // near_count, 3 * SHELLS, 128)
    )
    spectra = lax.all_to_all(spectra, NEAR, 0, 0, axis_index_groups=[NEAR_ORDER], tiled=True)
    spectra = lax.all_gather(spectra, "c", axis=0, tiled=True)
    coef = spectra.reshape(order_count, 2, 2, 3, SHELLS, 128).transpose(3, 0, 4, 1, 2, 5)
    coef = coef.reshape(3, order_count, SHELLS, 2, degree_dev)

    q, s, t = coef[0], coef[1], coef[2]
    swap = lambda v: jnp.stack([-v[:, :, 1], v[:, :, 0]], axis=2)
    theta = jnp.concatenate([s, swap(t)], axis=-1)
    phi = jnp.concatenate([-t, swap(s)], axis=-1)
    both = jnp.concatenate([theta, phi], axis=1)
    plain = jnp.einsum("mscl,mal->mcsa", q, plain_table, preferred_element_type=jnp.float32)
    pair = jnp.einsum("mscl,mal->mcsa", both, pair_table, preferred_element_type=jnp.float32)
    fourier = jnp.stack([plain, pair[:, :, :SHELLS], pair[:, :, SHELLS:]])
    fourier = fourier.transpose(3, 2, 1, 0, 4).reshape(SHELLS, 2 * order_count, -1)
    fourier = lax.all_to_all(
        fourier.astype(jnp.bfloat16), TAB, 0, 0, axis_index_groups=[TAB_ORDER], tiled=True
    )
    summed = jnp.sum(fourier.astype(jnp.float32), axis=0)
    f_hi, f_lo = split_bf16(summed)
    values = lax.dot_general(
        jnp.concatenate([f_hi, f_hi, f_lo]),
        jnp.concatenate([p_hi, p_lo, p_hi]),
        (((0,), (0,)), ((), ())),
        preferred_element_type=jnp.float32,
    )
    return values.astype(jnp.bfloat16).reshape(3, 1, -1, NPHI)


def solution(mesh):
    fine = Mesh(mesh.devices.reshape(2, 4, 2, 4, 4, 2), TAB + RAD)
    placed = (
        P(RAD, None, None, TAB),
        P(RAD, None, None, TAB),
        P(None, None, RAD, TAB),
        P(),
    )
    return jax.shard_map(
        on_device,
        mesh=fine,
        in_specs=placed,
        out_specs=P(None, TAB, RAD, None),
        check_vma=False,
    )
```

```python
import math

import jax
import jax.numpy as jnp
import numpy as np
from jax import lax
from jax.experimental import pallas as pl
from jax.experimental.pallas import tpu as pltpu
from jax.sharding import Mesh, PartitionSpec as P

NPHI = 6144
SHELLS = 8
RAD = ("xl", "zf", "zn", "c")
NEAR = ("xl", "zn")
NEAR_ORDER = (5, 6, 7, 4, 1, 2, 3, 0)
FAR_ORDER = (2, 3, 0, 1)
TAB_ORDER = (7, 6, 5, 4, 3, 2, 1, 0)
TAB = ("xh", "y")


def shell_radius():
    angle = math.pi / (2 * SHELLS) * (2 * np.array(TAB_ORDER) + 1)
    return (1.04 + 0.5 * np.cos(angle)).astype(np.float32)


def level_constants(level_dev):
    row = np.arange(2 * 3 * SHELLS)[:, None]
    col = np.arange(4 * level_dev * 2)[None, :]
    kind = row % (3 * SHELLS) // SHELLS
    odd = 2 * np.array(TAB_ORDER)[row % SHELLS] + 1
    source = col // (2 * level_dev)
    used = (row // (3 * SHELLS) == col % 2) & ((kind < 2) == (source < 2))
    step_angle = math.pi / (2 * SHELLS)
    planes = []
    for parity in range(4 * SHELLS // level_dev):
        level = parity * level_dev + col % (2 * level_dev) // 2
        angle = step_angle * (level * odd % (4 * SHELLS))
        value = np.where(used & (kind != 1), np.cos(angle), 0.0)
        slope = np.where(used & (kind == 1), 2.0 * np.sin(angle) / np.sin(step_angle * odd), 0.0)
        planes.append(np.stack([value, slope]))
    return np.stack(planes).astype(np.float32)


def level_kernel(
    constant_hbm, pol_hbm, tor_hbm, orders_hbm, out_ref, phase_ref, weight_ref,
    constant_ref, pol_ref, tor_ref, orders_ref, sems,
):
    loads = [
        pltpu.make_async_copy(source, target, sems.at[at])
        for at, (source, target) in enumerate(
            [
                (orders_hbm, orders_ref),
                (constant_hbm, constant_ref),
                (pol_hbm, pol_ref),
                (tor_hbm, tor_ref),
            ]
        )
    ]
    for load in loads:
        load.start()
    loads[0].wait()
    weight_rows(orders_ref, weight_ref)
    longitude_rows(orders_ref, phase_ref)
    for load in loads[1:]:
        load.wait()

    level_dev, order_count, _, degree_dev = pol_ref.shape
    rows = out_ref.shape[1]
    run = lax.axis_index(RAD)
    plane = lax.rem(run, constant_ref.shape[0])
    col = lax.broadcasted_iota(jnp.int32, constant_ref.shape[2:], 1)
    level = (run * level_dev + col % (2 * level_dev) // 2).astype(jnp.float32)
    entry = constant_ref[plane, 0] + level * constant_ref[plane, 1]
    high, low = halves(entry)
    matrix = jnp.where(col // (2 * level_dev) % 2 == 0, high, low)
    for order in range(order_count):
        pol = pol_ref[:, order].reshape(2 * level_dev, degree_dev)
        tor = tor_ref[:, order].reshape(2 * level_dev, degree_dev)
        sums = dot32(matrix, jnp.concatenate([pol, pol, tor, tor], axis=0))
        for part in range(2):
            for cut in range(degree_dev // 128):
                block = sums[part * rows : (part + 1) * rows, cut * 128 : (cut + 1) * 128]
                out_ref[(order * 2 + part) * (degree_dev // 128) + cut] = block.astype(jnp.bfloat16)


def halves(x):
    high = x.astype(jnp.bfloat16)
    return high, (x - high.astype(jnp.float32)).astype(jnp.bfloat16)


def weight_rows(orders_ref, weight_ref):
    order = orders_ref[own_order()]
    cut = lax.broadcasted_iota(jnp.int32, weight_ref.shape, 0)
    lane = lax.broadcasted_iota(jnp.int32, weight_ref.shape, 1)
    degree = (lax.axis_index(TAB) * weight_ref.shape[0] + cut) * weight_ref.shape[1] + lane
    degree_wide = degree.astype(jnp.float32)
    weight = jnp.sqrt(degree_wide * (degree_wide + 1.0))
    weight_ref[...] = jnp.where(degree >= order, weight, 0.0)


def longitude_rows(orders_ref, phase_ref):
    order_count = orders_ref.shape[0]
    points = phase_ref.shape[1]
    row = lax.broadcasted_iota(jnp.int32, (order_count, 128), 0)
    lane = lax.broadcasted_iota(jnp.int32, (order_count, 128), 1).astype(jnp.float32)
    order = jnp.zeros((order_count, 128), jnp.int32)
    for at in range(order_count):
        order = jnp.where(row == at, orders_ref[at], order)
    order = order.astype(jnp.float32)
    first = order * lane
    quarter = points // 4
    for start in range(0, points, 128):
        turn = first + order * float(start)
        quarters = jnp.floor(turn * (1.0 / quarter) + 0.5)
        x = (turn - quarters * float(quarter)) * (2.0 * math.pi / points)
        z = x * x
        sine = x * (1 + z * (-1 / 6 + z * (1 / 120 + z * (-1 / 5040 + z * (1 / 362880)))))
        cosine = 1 + z * (-1 / 2 + z * (1 / 24 + z * (-1 / 720 + z * (1 / 40320))))
        quarters = quarters.astype(jnp.int32)
        odd = (quarters & 1) == 1
        cos_row = jnp.where(odd, sine, cosine)
        sin_row = jnp.where(odd, cosine, sine)
        cos_row = jnp.where(((quarters + 1) & 2) == 0, 2.0, -2.0) * cos_row
        sin_row = jnp.where((quarters & 2) == 0, -2.0, 2.0) * sin_row
        cos_high, cos_low = halves(cos_row)
        sin_high, sin_low = halves(sin_row)
        for at, rows in enumerate([cos_high, sin_high, cos_low, sin_low, cos_high, sin_high]):
            phase_ref[at * order_count : (at + 1) * order_count, start : start + 128] = rows


def near_place():
    return (1 - lax.axis_index("xl")) * 4 + lax.rem(lax.axis_index("zn") + 3, 4)


def own_order():
    return lax.axis_index("c") * len(NEAR_ORDER) + near_place()


def level_sums(poloidal, toroidal, orders):
    level_dev, order_count, _, degree_dev = poloidal.shape
    constants = level_constants(level_dev)
    return pl.pallas_call(
        level_kernel,
        out_shape=(
            pltpu.VMEM((order_count * 2 * degree_dev // 128, 3 * SHELLS, 128), jnp.bfloat16),
            pltpu.VMEM((6 * order_count, NPHI), jnp.bfloat16),
            pltpu.VMEM((degree_dev // 128, 128), jnp.float32),
        ),
        in_specs=[pl.BlockSpec(memory_space=pltpu.HBM)] * 4,
        out_specs=[pl.BlockSpec(memory_space=pltpu.VMEM)] * 3,
        scratch_shapes=[
            pltpu.VMEM(constants.shape, jnp.float32),
            pltpu.VMEM(poloidal.shape, jnp.bfloat16),
            pltpu.VMEM(toroidal.shape, jnp.bfloat16),
            pltpu.SMEM(orders.shape, jnp.int32),
            pltpu.SemaphoreType.DMA((4,)),
        ],
        compiler_params=pltpu.CompilerParams(vmem_limit_bytes=57_000_000),
        name="level_sums",
    )(constants, poloidal, toroidal, orders)


def split_bf16(x):
    hi = lax.reduce_precision(x, 8, 7)
    return hi.astype(jnp.bfloat16), (x - hi).astype(jnp.bfloat16)


def dot32(a, b):
    return jnp.dot(a, b, preferred_element_type=jnp.float32)


def on_device(poloidal, toroidal, tables, orders):
    _, order_count, _, degree_dev = poloidal.shape
    half = order_count // 2
    blocks = half * 2 * degree_dev // 128
    near_count = lax.axis_size(NEAR)
    far_count = lax.axis_size("zf")
    first_block = lax.axis_index("c") * blocks
    partial, phases, weight = level_sums(poloidal, toroidal, orders)
    pair = lax.all_gather(partial, "c", axis=0)
    pair = lax.dynamic_slice_in_dim(pair, first_block, blocks, 1).astype(jnp.float32)
    partial = (pair[0] + pair[1]).astype(jnp.bfloat16)
    shares = lax.all_to_all(partial, NEAR, 0, 0, axis_index_groups=[NEAR_ORDER], tiled=True)
    shares = shares.reshape(near_count, -1, 3 * SHELLS, 128).astype(jnp.float32)
    near_sum, tables = lax.optimization_barrier((jnp.sum(shares, axis=0), tables))
    copies = jnp.broadcast_to(near_sum.astype(jnp.bfloat16), (far_count,) + near_sum.shape)
    pair_table = jnp.concatenate([tables[1], tables[2]], axis=-1)
    copies, plain_table, pair_table = lax.optimization_barrier((copies, tables[0], pair_table))
    shares = lax.all_to_all(copies, "zf", 0, 0, axis_index_groups=[FAR_ORDER], tiled=True)
    radial = jnp.sum(shares.astype(jnp.float32), axis=0)
    radial = radial.reshape(2, degree_dev // 128, 3, SHELLS, 128)
    weight = weight.reshape(1, degree_dev // 128, 1, 128)
    spheroidal = radial[:, :, 0] / shell_radius()[:, None]
    spectra = jnp.stack(
        [
            weight * spheroidal,
            weight * (spheroidal + radial[:, :, 1]),
            weight * radial[:, :, 2],
        ],
        axis=2,
    ).astype(jnp.bfloat16)
    spectra = jnp.broadcast_to(
        spectra.reshape(1, -1, 3 * SHELLS, 128), (near_count, blocks // near_count, 3 * SHELLS, 128)
    )
    spectra = lax.all_to_all(spectra, NEAR, 0, 0, axis_index_groups=[NEAR_ORDER], tiled=True)
    spectra = lax.all_gather(spectra, "c", axis=0, tiled=True)
    coef = spectra.reshape(order_count, 2, 2, 3, SHELLS, 128).transpose(3, 0, 4, 1, 2, 5)
    coef = coef.reshape(3, order_count, SHELLS, 2, degree_dev)

    q, s, t = coef[0], coef[1], coef[2]
    swap = lambda v: jnp.stack([-v[:, :, 1], v[:, :, 0]], axis=2)
    theta = jnp.concatenate([s, swap(t)], axis=-1)
    phi = jnp.concatenate([-t, swap(s)], axis=-1)
    both = jnp.concatenate([theta, phi], axis=1)
    plain = jnp.einsum("mscl,mal->mcsa", q, plain_table, preferred_element_type=jnp.float32)
    pair = jnp.einsum("mscl,mal->mcsa", both, pair_table, preferred_element_type=jnp.float32)
    fourier = jnp.stack([plain, pair[:, :, :SHELLS], pair[:, :, SHELLS:]])
    fourier = fourier.transpose(3, 2, 1, 0, 4).reshape(SHELLS, 2 * order_count, -1)
    fourier = lax.all_to_all(
        fourier.astype(jnp.bfloat16), TAB, 0, 0, axis_index_groups=[TAB_ORDER], tiled=True
    )
    summed = jnp.sum(fourier.astype(jnp.float32), axis=0)
    f_hi, f_lo = split_bf16(summed)
    values = lax.dot_general(
        jnp.concatenate([f_hi, f_hi, f_lo]),
        phases,
        (((0,), (0,)), ((), ())),
        preferred_element_type=jnp.float32,
    )
    return values.astype(jnp.bfloat16).reshape(3, 1, -1, NPHI)


def solution(mesh):
    fine = Mesh(mesh.devices.reshape(2, 4, 2, 4, 4, 2), TAB + RAD)
    placed = (
        P(RAD, None, None, TAB),
        P(RAD, None, None, TAB),
        P(None, None, RAD, TAB),
        P(),
    )
    return jax.shard_map(
        on_device,
        mesh=fine,
        in_specs=placed,
        out_specs=P(None, TAB, RAD, None),
        check_vma=False,
    )
```

```python
import math

import jax
import jax.numpy as jnp
import numpy as np
from jax import lax
from jax.experimental import pallas as pl
from jax.experimental.pallas import tpu as pltpu
from jax.sharding import Mesh, PartitionSpec as P

NPHI = 6144
SHELLS = 8
RAD = ("xl", "zf", "zn", "c")
NEAR = ("xl", "zn")
NEAR_ORDER = (5, 6, 7, 4, 1, 2, 3, 0)
FAR_ORDER = (2, 3, 0, 1)
TAB_ORDER = (6, 2, 7, 3, 5, 1, 4, 0)
TAB = ("xh", "y")


def shell_radius():
    angle = math.pi / (2 * SHELLS) * (2 * np.array(TAB_ORDER) + 1)
    return (1.04 + 0.5 * np.cos(angle)).astype(np.float32)


def level_constants(level_dev):
    row = np.arange(2 * 3 * SHELLS)[:, None]
    col = np.arange(4 * level_dev * 2)[None, :]
    kind = row % (3 * SHELLS) // SHELLS
    odd = 2 * np.array(TAB_ORDER)[row % SHELLS] + 1
    source = col // (2 * level_dev)
    used = (row // (3 * SHELLS) == col % 2) & ((kind < 2) == (source < 2))
    step_angle = math.pi / (2 * SHELLS)
    planes = []
    for parity in range(4 * SHELLS // level_dev):
        level = parity * level_dev + col % (2 * level_dev) // 2
        angle = step_angle * (level * odd % (4 * SHELLS))
        value = np.where(used & (kind != 1), np.cos(angle), 0.0)
        slope = np.where(used & (kind == 1), 2.0 * np.sin(angle) / np.sin(step_angle * odd), 0.0)
        planes.append(np.stack([value, slope]))
    return np.stack(planes).astype(np.float32)


def level_kernel(
    constant_hbm, pol_hbm, tor_hbm, orders_hbm, out_ref, phase_ref, weight_ref,
    constant_ref, pol_ref, tor_ref, orders_ref, sems,
):
    loads = [
        pltpu.make_async_copy(source, target, sems.at[at])
        for at, (source, target) in enumerate(
            [
                (orders_hbm, orders_ref),
                (constant_hbm, constant_ref),
                (pol_hbm, pol_ref),
                (tor_hbm, tor_ref),
            ]
        )
    ]
    for load in loads:
        load.start()
    loads[0].wait()
    weight_rows(orders_ref, weight_ref)
    longitude_rows(orders_ref, phase_ref)
    for load in loads[1:]:
        load.wait()

    level_dev, order_count, _, degree_dev = pol_ref.shape
    rows = out_ref.shape[1]
    run = lax.axis_index(RAD)
    plane = lax.rem(run, constant_ref.shape[0])
    col = lax.broadcasted_iota(jnp.int32, constant_ref.shape[2:], 1)
    level = (run * level_dev + col % (2 * level_dev) // 2).astype(jnp.float32)
    entry = constant_ref[plane, 0] + level * constant_ref[plane, 1]
    high, low = halves(entry)
    matrix = jnp.where(col // (2 * level_dev) % 2 == 0, high, low)
    for order in range(order_count):
        pol = pol_ref[:, order].reshape(2 * level_dev, degree_dev)
        tor = tor_ref[:, order].reshape(2 * level_dev, degree_dev)
        sums = dot32(matrix, jnp.concatenate([pol, pol, tor, tor], axis=0))
        for part in range(2):
            for cut in range(degree_dev // 128):
                block = sums[part * rows : (part + 1) * rows, cut * 128 : (cut + 1) * 128]
                out_ref[(order * 2 + part) * (degree_dev // 128) + cut] = block.astype(jnp.bfloat16)


def halves(x):
    high = x.astype(jnp.bfloat16)
    return high, (x - high.astype(jnp.float32)).astype(jnp.bfloat16)


def weight_rows(orders_ref, weight_ref):
    order = orders_ref[own_order()]
    cut = lax.broadcasted_iota(jnp.int32, weight_ref.shape, 0)
    lane = lax.broadcasted_iota(jnp.int32, weight_ref.shape, 1)
    degree = (lax.axis_index(TAB) * weight_ref.shape[0] + cut) * weight_ref.shape[1] + lane
    degree_wide = degree.astype(jnp.float32)
    weight = jnp.sqrt(degree_wide * (degree_wide + 1.0))
    weight_ref[...] = jnp.where(degree >= order, weight, 0.0)


def longitude_rows(orders_ref, phase_ref):
    order_count = orders_ref.shape[0]
    points = phase_ref.shape[1]
    row = lax.broadcasted_iota(jnp.int32, (order_count, 128), 0)
    lane = lax.broadcasted_iota(jnp.int32, (order_count, 128), 1).astype(jnp.float32)
    order = jnp.zeros((order_count, 128), jnp.int32)
    for at in range(order_count):
        order = jnp.where(row == at, orders_ref[at], order)
    order = order.astype(jnp.float32)
    first = order * lane
    quarter = points // 4
    for start in range(0, points, 128):
        turn = first + order * float(start)
        quarters = jnp.floor(turn * (1.0 / quarter) + 0.5)
        x = (turn - quarters * float(quarter)) * (2.0 * math.pi / points)
        z = x * x
        sine = x * (1 + z * (-1 / 6 + z * (1 / 120 + z * (-1 / 5040 + z * (1 / 362880)))))
        cosine = 1 + z * (-1 / 2 + z * (1 / 24 + z * (-1 / 720 + z * (1 / 40320))))
        quarters = quarters.astype(jnp.int32)
        odd = (quarters & 1) == 1
        cos_row = jnp.where(odd, sine, cosine)
        sin_row = jnp.where(odd, cosine, sine)
        cos_row = jnp.where(((quarters + 1) & 2) == 0, 2.0, -2.0) * cos_row
        sin_row = jnp.where((quarters & 2) == 0, -2.0, 2.0) * sin_row
        cos_high, cos_low = halves(cos_row)
        sin_high, sin_low = halves(sin_row)
        for at, rows in enumerate([cos_high, sin_high, cos_low, sin_low, cos_high, sin_high]):
            phase_ref[at * order_count : (at + 1) * order_count, start : start + 128] = rows


def near_place():
    return (1 - lax.axis_index("xl")) * 4 + lax.rem(lax.axis_index("zn") + 3, 4)


def own_order():
    return lax.axis_index("c") * len(NEAR_ORDER) + near_place()


def level_sums(poloidal, toroidal, orders):
    level_dev, order_count, _, degree_dev = poloidal.shape
    constants = level_constants(level_dev)
    return pl.pallas_call(
        level_kernel,
        out_shape=(
            pltpu.VMEM((order_count * 2 * degree_dev // 128, 3 * SHELLS, 128), jnp.bfloat16),
            pltpu.VMEM((6 * order_count, NPHI), jnp.bfloat16),
            pltpu.VMEM((degree_dev // 128, 128), jnp.float32),
        ),
        in_specs=[pl.BlockSpec(memory_space=pltpu.HBM)] * 4,
        out_specs=[pl.BlockSpec(memory_space=pltpu.VMEM)] * 3,
        scratch_shapes=[
            pltpu.VMEM(constants.shape, jnp.float32),
            pltpu.VMEM(poloidal.shape, jnp.bfloat16),
            pltpu.VMEM(toroidal.shape, jnp.bfloat16),
            pltpu.SMEM(orders.shape, jnp.int32),
            pltpu.SemaphoreType.DMA((4,)),
        ],
        compiler_params=pltpu.CompilerParams(vmem_limit_bytes=57_000_000),
        name="level_sums",
    )(constants, poloidal, toroidal, orders)


def dot32(a, b):
    return jnp.dot(a, b, preferred_element_type=jnp.float32)


def synthesis_kernel(share_ref, phase_ref, out_hbm, chunk_ref, sems):
    chunks, _, width = chunk_ref.shape
    high, low = halves(jnp.sum(share_ref[...].astype(jnp.float32), axis=0))
    rows = jnp.concatenate([high, high, low], axis=0)
    copies = []
    for at in range(chunks):
        columns = slice(at * width, (at + 1) * width)
        values = lax.dot_general(
            rows,
            phase_ref[:, columns],
            (((0,), (0,)), ((), ())),
            preferred_element_type=jnp.float32,
        )
        chunk_ref[at] = values.astype(jnp.bfloat16)
        copies.append(
            pltpu.make_async_copy(chunk_ref.at[at], out_hbm.at[:, columns], sems.at[at])
        )
        copies[-1].start()
    for copy in copies:
        copy.wait()


def synthesis(shares, phases, chunks):
    rows, points = shares.shape[2], phases.shape[1]
    return pl.pallas_call(
        synthesis_kernel,
        out_shape=jax.ShapeDtypeStruct((rows, points), jnp.bfloat16),
        in_specs=[pl.BlockSpec(memory_space=pltpu.VMEM)] * 2,
        out_specs=pl.BlockSpec(memory_space=pltpu.HBM),
        scratch_shapes=[
            pltpu.VMEM((chunks, rows, points // chunks), jnp.bfloat16),
            pltpu.SemaphoreType.DMA((chunks,)),
        ],
        compiler_params=pltpu.CompilerParams(vmem_limit_bytes=16 << 20),
        name="synthesis",
    )(shares, phases)


def on_device(poloidal, toroidal, tables, orders):
    _, order_count, _, degree_dev = poloidal.shape
    half = order_count // 2
    blocks = half * 2 * degree_dev // 128
    near_count = lax.axis_size(NEAR)
    far_count = lax.axis_size("zf")
    first_block = lax.axis_index("c") * blocks
    partial, phases, weight = level_sums(poloidal, toroidal, orders)
    pair = lax.all_gather(partial, "c", axis=0)
    pair = lax.dynamic_slice_in_dim(pair, first_block, blocks, 1).astype(jnp.float32)
    partial = (pair[0] + pair[1]).astype(jnp.bfloat16)
    shares = lax.all_to_all(partial, NEAR, 0, 0, axis_index_groups=[NEAR_ORDER], tiled=True)
    shares = shares.reshape(near_count, -1, 3 * SHELLS, 128).astype(jnp.float32)
    near_sum, tables = lax.optimization_barrier((jnp.sum(shares, axis=0), tables))
    copies = jnp.broadcast_to(near_sum.astype(jnp.bfloat16), (far_count,) + near_sum.shape)
    pair_table = jnp.concatenate([tables[1], tables[2]], axis=-1)
    copies, plain_table, pair_table = lax.optimization_barrier((copies, tables[0], pair_table))
    shares = lax.all_to_all(copies, "zf", 0, 0, axis_index_groups=[FAR_ORDER], tiled=True)
    radial = jnp.sum(shares.astype(jnp.float32), axis=0)
    radial = radial.reshape(2, degree_dev // 128, 3, SHELLS, 128)
    weight = weight.reshape(1, degree_dev // 128, 1, 128)
    spheroidal = radial[:, :, 0] / shell_radius()[:, None]
    spectra = jnp.stack(
        [
            weight * spheroidal,
            weight * (spheroidal + radial[:, :, 1]),
            weight * radial[:, :, 2],
        ],
        axis=2,
    ).astype(jnp.bfloat16)
    spectra = jnp.broadcast_to(
        spectra.reshape(1, -1, 3 * SHELLS, 128), (near_count, blocks // near_count, 3 * SHELLS, 128)
    )
    spectra = lax.all_to_all(spectra, NEAR, 0, 0, axis_index_groups=[NEAR_ORDER], tiled=True)
    spectra = lax.all_gather(spectra, "c", axis=0, tiled=True)
    coef = spectra.reshape(order_count, 2, 2, 3, SHELLS, 128).transpose(3, 0, 4, 1, 2, 5)
    coef = coef.reshape(3, order_count, SHELLS, 2, degree_dev)

    q, s, t = coef[0], coef[1], coef[2]
    swap = lambda v: jnp.stack([-v[:, :, 1], v[:, :, 0]], axis=2)
    theta = jnp.concatenate([s, swap(t)], axis=-1)
    phi = jnp.concatenate([-t, swap(s)], axis=-1)
    both = jnp.concatenate([theta, phi], axis=1)
    plain = jnp.einsum("mscl,mal->mcsa", q, plain_table, preferred_element_type=jnp.float32)
    pair = jnp.einsum("mscl,mal->mcsa", both, pair_table, preferred_element_type=jnp.float32)
    fourier = jnp.stack([plain, pair[:, :, :SHELLS], pair[:, :, SHELLS:]])
    fourier = fourier.transpose(3, 2, 1, 0, 4).reshape(SHELLS, 2 * order_count, -1)
    fourier = lax.all_to_all(
        fourier.astype(jnp.bfloat16), TAB, 0, 0, axis_index_groups=[TAB_ORDER], tiled=True
    )
    return synthesis(fourier, phases, 4).reshape(3, 1, -1, NPHI)


def solution(mesh):
    fine = Mesh(mesh.devices.reshape(2, 4, 2, 4, 4, 2), TAB + RAD)
    placed = (
        P(RAD, None, None, TAB),
        P(RAD, None, None, TAB),
        P(None, None, RAD, TAB),
        P(),
    )
    return jax.shard_map(
        on_device,
        mesh=fine,
        in_specs=placed,
        out_specs=P(None, TAB, RAD, None),
        check_vma=False,
    )
```

```python
import math

import jax
import jax.numpy as jnp
import numpy as np
from jax import lax
from jax.experimental import pallas as pl
from jax.experimental.pallas import tpu as pltpu
from jax.sharding import Mesh, PartitionSpec as P

NPHI = 6144
SHELLS = 8
RAD = ("xl", "zf", "zn", "c")
NEAR = ("xl", "zn")
NEAR_ORDER = (5, 6, 7, 4, 1, 2, 3, 0)
FAR_ORDER = (2, 3, 0, 1)
TAB_ORDER = (6, 2, 7, 3, 5, 1, 4, 0)
TAB = ("xh", "y")


def shell_radius():
    angle = math.pi / (2 * SHELLS) * (2 * np.array(TAB_ORDER) + 1)
    return (1.04 + 0.5 * np.cos(angle)).astype(np.float32)


def level_constants(level_dev):
    row = np.arange(2 * 3 * SHELLS)[:, None]
    col = np.arange(4 * level_dev * 2)[None, :]
    kind = row % (3 * SHELLS) // SHELLS
    odd = 2 * np.array(TAB_ORDER)[row % SHELLS] + 1
    source = col // (2 * level_dev)
    used = (row // (3 * SHELLS) == col % 2) & ((kind < 2) == (source < 2))
    step_angle = math.pi / (2 * SHELLS)
    planes = []
    for parity in range(4 * SHELLS // level_dev):
        level = parity * level_dev + col % (2 * level_dev) // 2
        angle = step_angle * (level * odd % (4 * SHELLS))
        value = np.where(used & (kind != 1), np.cos(angle), 0.0)
        slope = np.where(used & (kind == 1), 2.0 * np.sin(angle) / np.sin(step_angle * odd), 0.0)
        planes.append(np.stack([value, slope]))
    return np.stack(planes).astype(np.float32)


def level_kernel(
    constant_hbm, pol_hbm, tor_hbm, orders_hbm, out_ref, phase_ref, weight_ref,
    constant_ref, pol_ref, tor_ref, orders_ref, sems,
):
    loads = [
        pltpu.make_async_copy(source, target, sems.at[at])
        for at, (source, target) in enumerate(
            [
                (orders_hbm, orders_ref),
                (constant_hbm, constant_ref),
                (pol_hbm, pol_ref),
                (tor_hbm, tor_ref),
            ]
        )
    ]
    for load in loads:
        load.start()
    loads[0].wait()
    weight_rows(orders_ref, weight_ref)
    longitude_rows(orders_ref, phase_ref)
    for load in loads[1:]:
        load.wait()

    level_dev, order_count, _, degree_dev = pol_ref.shape
    rows = out_ref.shape[1]
    run = lax.axis_index(RAD)
    plane = lax.rem(run, constant_ref.shape[0])
    col = lax.broadcasted_iota(jnp.int32, constant_ref.shape[2:], 1)
    level = (run * level_dev + col % (2 * level_dev) // 2).astype(jnp.float32)
    entry = constant_ref[plane, 0] + level * constant_ref[plane, 1]
    high, low = halves(entry)
    matrix = jnp.where(col // (2 * level_dev) % 2 == 0, high, low)
    for order in range(order_count):
        pol = pol_ref[:, order].reshape(2 * level_dev, degree_dev)
        tor = tor_ref[:, order].reshape(2 * level_dev, degree_dev)
        sums = dot32(matrix, jnp.concatenate([pol, pol, tor, tor], axis=0))
        for part in range(2):
            for cut in range(degree_dev // 128):
                block = sums[part * rows : (part + 1) * rows, cut * 128 : (cut + 1) * 128]
                out_ref[(order * 2 + part) * (degree_dev // 128) + cut] = block.astype(jnp.bfloat16)


def halves(x):
    high = x.astype(jnp.bfloat16)
    return high, (x - high.astype(jnp.float32)).astype(jnp.bfloat16)


def weight_rows(orders_ref, weight_ref):
    order = orders_ref[own_order()]
    cut = lax.broadcasted_iota(jnp.int32, weight_ref.shape, 0)
    lane = lax.broadcasted_iota(jnp.int32, weight_ref.shape, 1)
    degree = (lax.axis_index(TAB) * weight_ref.shape[0] + cut) * weight_ref.shape[1] + lane
    degree_wide = degree.astype(jnp.float32)
    weight = jnp.sqrt(degree_wide * (degree_wide + 1.0))
    weight_ref[...] = jnp.where(degree >= order, weight, 0.0)


def longitude_rows(orders_ref, phase_ref):
    order_count = orders_ref.shape[0]
    points = phase_ref.shape[1]
    row = lax.broadcasted_iota(jnp.int32, (order_count, 128), 0)
    lane = lax.broadcasted_iota(jnp.int32, (order_count, 128), 1).astype(jnp.float32)
    order = jnp.zeros((order_count, 128), jnp.int32)
    for at in range(order_count):
        order = jnp.where(row == at, orders_ref[at], order)
    order = order.astype(jnp.float32)
    first = order * lane
    quarter = points // 4
    for start in range(0, points, 128):
        turn = first + order * float(start)
        quarters = jnp.floor(turn * (1.0 / quarter) + 0.5)
        x = (turn - quarters * float(quarter)) * (2.0 * math.pi / points)
        z = x * x
        sine = x * (1 + z * (-1 / 6 + z * (1 / 120 + z * (-1 / 5040 + z * (1 / 362880)))))
        cosine = 1 + z * (-1 / 2 + z * (1 / 24 + z * (-1 / 720 + z * (1 / 40320))))
        quarters = quarters.astype(jnp.int32)
        odd = (quarters & 1) == 1
        cos_row = jnp.where(odd, sine, cosine)
        sin_row = jnp.where(odd, cosine, sine)
        cos_row = jnp.where(((quarters + 1) & 2) == 0, 2.0, -2.0) * cos_row
        sin_row = jnp.where((quarters & 2) == 0, -2.0, 2.0) * sin_row
        cos_high, cos_low = halves(cos_row)
        sin_high, sin_low = halves(sin_row)
        for at, rows in enumerate([cos_high, sin_high, cos_low, sin_low, cos_high, sin_high]):
            phase_ref[at * order_count : (at + 1) * order_count, start : start + 128] = rows


def near_place():
    return (1 - lax.axis_index("xl")) * 4 + lax.rem(lax.axis_index("zn") + 3, 4)


def own_order():
    return lax.axis_index("c") * len(NEAR_ORDER) + near_place()


def level_sums(poloidal, toroidal, orders):
    level_dev, order_count, _, degree_dev = poloidal.shape
    constants = level_constants(level_dev)
    return pl.pallas_call(
        level_kernel,
        out_shape=(
            pltpu.VMEM((order_count * 2 * degree_dev // 128, 3 * SHELLS, 128), jnp.bfloat16),
            pltpu.VMEM((6 * order_count, NPHI), jnp.bfloat16),
            pltpu.VMEM((degree_dev // 128, 128), jnp.float32),
        ),
        in_specs=[pl.BlockSpec(memory_space=pltpu.HBM)] * 4,
        out_specs=[pl.BlockSpec(memory_space=pltpu.VMEM)] * 3,
        scratch_shapes=[
            pltpu.VMEM(constants.shape, jnp.float32),
            pltpu.VMEM(poloidal.shape, jnp.bfloat16),
            pltpu.VMEM(toroidal.shape, jnp.bfloat16),
            pltpu.SMEM(orders.shape, jnp.int32),
            pltpu.SemaphoreType.DMA((4,)),
        ],
        compiler_params=pltpu.CompilerParams(vmem_limit_bytes=57_000_000),
        name="level_sums",
    )(constants, poloidal, toroidal, orders)


def dot32(a, b):
    return jnp.dot(a, b, preferred_element_type=jnp.float32)


def projection_kernel(spectra_ref, table_ref, out_ref, held_ref):
    order_count = table_ref.shape[1]
    cuts = spectra_ref.shape[1] // 2

    def project(rows, table):
        return lax.dot_general(
            jnp.concatenate(rows, axis=0).astype(jnp.bfloat16),
            table,
            (((1,), (1,)), ((), ())),
            preferred_element_type=jnp.float32,
        )

    for order in range(order_count):
        blocks = [spectra_ref[order, at].astype(jnp.float32) for at in range(2 * cuts)]
        (q_re, q_im), (s_re, s_im), (t_re, t_im) = (
            [
                jnp.concatenate(
                    [
                        block[kind * SHELLS : (kind + 1) * SHELLS]
                        for block in blocks[part * cuts : (part + 1) * cuts]
                    ],
                    axis=1,
                )
                for part in range(2)
            ]
            for kind in range(3)
        )
        held_ref[0, order] = project([q_re, q_im], table_ref[0, order])
        pair = project([s_re, s_im, -t_re, -t_im], table_ref[1, order])
        pair += project([-t_im, t_re, -s_im, s_re], table_ref[2, order])
        held_ref[1, order] = pair[: 2 * SHELLS]
        held_ref[2, order] = pair[2 * SHELLS :]
    for shell in range(SHELLS):
        for part in range(2):
            rows = [held_ref[kind, :, part * SHELLS + shell, :] for kind in range(3)]
            out_ref[shell, part * order_count : (part + 1) * order_count, :] = jnp.concatenate(
                rows, axis=1
            ).astype(jnp.bfloat16)


def projection(spectra, tables):
    kinds, order_count, latitudes, _ = tables.shape
    return pl.pallas_call(
        projection_kernel,
        out_shape=pltpu.VMEM((SHELLS, 2 * order_count, kinds * latitudes), jnp.bfloat16),
        in_specs=[pl.BlockSpec(memory_space=pltpu.VMEM)] * 2,
        out_specs=pl.BlockSpec(memory_space=pltpu.VMEM),
        scratch_shapes=[pltpu.VMEM((kinds, order_count, 2 * SHELLS, latitudes), jnp.float32)],
        compiler_params=pltpu.CompilerParams(vmem_limit_bytes=16 << 20),
        name="projection",
    )(spectra, tables)


def synthesis_kernel(share_ref, phase_ref, out_hbm, chunk_ref, sems):
    chunks, _, width = chunk_ref.shape
    high, low = halves(jnp.sum(share_ref[...].astype(jnp.float32), axis=0))
    rows = jnp.concatenate([high, high, low], axis=0)
    copies = []
    for at in range(chunks):
        columns = slice(at * width, (at + 1) * width)
        values = lax.dot_general(
            rows,
            phase_ref[:, columns],
            (((0,), (0,)), ((), ())),
            preferred_element_type=jnp.float32,
        )
        chunk_ref[at] = values.astype(jnp.bfloat16)
        copies.append(
            pltpu.make_async_copy(chunk_ref.at[at], out_hbm.at[:, columns], sems.at[at])
        )
        copies[-1].start()
    for copy in copies:
        copy.wait()


def synthesis(shares, phases, chunks):
    rows, points = shares.shape[2], phases.shape[1]
    return pl.pallas_call(
        synthesis_kernel,
        out_shape=jax.ShapeDtypeStruct((rows, points), jnp.bfloat16),
        in_specs=[pl.BlockSpec(memory_space=pltpu.VMEM)] * 2,
        out_specs=pl.BlockSpec(memory_space=pltpu.HBM),
        scratch_shapes=[
            pltpu.VMEM((chunks, rows, points // chunks), jnp.bfloat16),
            pltpu.SemaphoreType.DMA((chunks,)),
        ],
        compiler_params=pltpu.CompilerParams(vmem_limit_bytes=16 << 20),
        name="synthesis",
    )(shares, phases)


def on_device(poloidal, toroidal, tables, orders):
    _, order_count, _, degree_dev = poloidal.shape
    half = order_count // 2
    blocks = half * 2 * degree_dev // 128
    near_count = lax.axis_size(NEAR)
    far_count = lax.axis_size("zf")
    first_block = lax.axis_index("c") * blocks
    partial, phases, weight = level_sums(poloidal, toroidal, orders)
    pair = lax.all_gather(partial, "c", axis=0)
    pair = lax.dynamic_slice_in_dim(pair, first_block, blocks, 1).astype(jnp.float32)
    partial = (pair[0] + pair[1]).astype(jnp.bfloat16)
    shares = lax.all_to_all(partial, NEAR, 0, 0, axis_index_groups=[NEAR_ORDER], tiled=True)
    shares = shares.reshape(near_count, -1, 3 * SHELLS, 128).astype(jnp.float32)
    near_sum = lax.optimization_barrier(jnp.sum(shares, axis=0))
    copies = jnp.broadcast_to(near_sum.astype(jnp.bfloat16), (far_count,) + near_sum.shape)
    shares = lax.all_to_all(copies, "zf", 0, 0, axis_index_groups=[FAR_ORDER], tiled=True)
    radial = jnp.sum(shares.astype(jnp.float32), axis=0)
    radial = radial.reshape(2, degree_dev // 128, 3, SHELLS, 128)
    weight = weight.reshape(1, degree_dev // 128, 1, 128)
    spheroidal = radial[:, :, 0] / shell_radius()[:, None]
    spectra = jnp.stack(
        [
            weight * spheroidal,
            weight * (spheroidal + radial[:, :, 1]),
            weight * radial[:, :, 2],
        ],
        axis=2,
    ).astype(jnp.bfloat16)
    spectra = jnp.broadcast_to(
        spectra.reshape(1, -1, 3 * SHELLS, 128), (near_count, blocks // near_count, 3 * SHELLS, 128)
    )
    spectra = lax.all_to_all(spectra, NEAR, 0, 0, axis_index_groups=[NEAR_ORDER], tiled=True)
    spectra = lax.all_gather(spectra, "c", axis=0, tiled=True)
    fourier = projection(spectra.reshape(order_count, -1, 3 * SHELLS, 128), tables)
    fourier = lax.all_to_all(fourier, TAB, 0, 0, axis_index_groups=[TAB_ORDER], tiled=True)
    return synthesis(fourier, phases, 4).reshape(3, 1, -1, NPHI)


def solution(mesh):
    fine = Mesh(mesh.devices.reshape(2, 4, 2, 4, 4, 2), TAB + RAD)
    placed = (
        P(RAD, None, None, TAB),
        P(RAD, None, None, TAB),
        P(None, None, RAD, TAB),
        P(),
    )
    return jax.shard_map(
        on_device,
        mesh=fine,
        in_specs=placed,
        out_specs=P(None, TAB, RAD, None),
        check_vma=False,
    )
```

```python
import math

import jax
import jax.numpy as jnp
import numpy as np
from jax import lax
from jax.experimental import pallas as pl
from jax.experimental.pallas import tpu as pltpu
from jax.sharding import Mesh, PartitionSpec as P

NPHI = 6144
SHELLS = 8
RAD = ("xl", "zf", "zn", "c")
NEAR = ("xl", "zn")
NEAR_ORDER = (5, 6, 7, 4, 1, 2, 3, 0)
FAR_ORDER = (2, 3, 0, 1)
TAB_ORDER = (6, 2, 7, 3, 5, 1, 4, 0)
TAB = ("xh", "y")


def shell_radius():
    angle = math.pi / (2 * SHELLS) * (2 * np.array(TAB_ORDER) + 1)
    return (1.04 + 0.5 * np.cos(angle)).astype(np.float32)


def level_constants(level_dev):
    row = np.arange(2 * 3 * SHELLS)[:, None]
    col = np.arange(4 * level_dev * 2)[None, :]
    kind = row % (3 * SHELLS) // SHELLS
    odd = 2 * np.array(TAB_ORDER)[row % SHELLS] + 1
    source = col // (2 * level_dev)
    used = (row // (3 * SHELLS) == col % 2) & ((kind < 2) == (source < 2))
    step_angle = math.pi / (2 * SHELLS)
    planes = []
    for parity in range(4 * SHELLS // level_dev):
        level = parity * level_dev + col % (2 * level_dev) // 2
        angle = step_angle * (level * odd % (4 * SHELLS))
        value = np.where(used & (kind != 1), np.cos(angle), 0.0)
        slope = np.where(used & (kind == 1), 2.0 * np.sin(angle) / np.sin(step_angle * odd), 0.0)
        planes.append(np.stack([value, slope]))
    return np.stack(planes).astype(np.float32)


def level_kernel(
    constant_hbm, pol_hbm, tor_hbm, orders_hbm, out_ref, own_ref, phase_ref, weight_ref,
    constant_ref, pol_ref, tor_ref, orders_ref, sems,
):
    loads = [
        pltpu.make_async_copy(source, target, sems.at[at])
        for at, (source, target) in enumerate(
            [
                (orders_hbm, orders_ref),
                (constant_hbm, constant_ref),
                (pol_hbm, pol_ref),
                (tor_hbm, tor_ref),
            ]
        )
    ]
    for load in loads:
        load.start()
    loads[0].wait()
    weight_rows(orders_ref, weight_ref)
    longitude_rows(orders_ref, phase_ref)
    for load in loads[1:]:
        load.wait()

    level_dev, order_count, _, degree_dev = pol_ref.shape
    rows = out_ref.shape[1]
    run = lax.axis_index(RAD)
    plane = lax.rem(run, constant_ref.shape[0])
    col = lax.broadcasted_iota(jnp.int32, constant_ref.shape[2:], 1)
    level = (run * level_dev + col % (2 * level_dev) // 2).astype(jnp.float32)
    entry = constant_ref[plane, 0] + level * constant_ref[plane, 1]
    high, low = halves(entry)
    matrix = jnp.where(col // (2 * level_dev) % 2 == 0, high, low)
    for order in range(order_count):
        pol = pol_ref[:, order].reshape(2 * level_dev, degree_dev)
        tor = tor_ref[:, order].reshape(2 * level_dev, degree_dev)
        sums = dot32(matrix, jnp.concatenate([pol, pol, tor, tor], axis=0))
        for part in range(2):
            for cut in range(degree_dev // 128):
                block = sums[part * rows : (part + 1) * rows, cut * 128 : (cut + 1) * 128]
                at = (order * 2 + part) * (degree_dev // 128) + cut
                out_ref[at] = block.astype(jnp.bfloat16)
                own_ref[at] = block


def halves(x):
    high = x.astype(jnp.bfloat16)
    return high, (x - high.astype(jnp.float32)).astype(jnp.bfloat16)


def weight_rows(orders_ref, weight_ref):
    order = orders_ref[own_order()]
    cut = lax.broadcasted_iota(jnp.int32, weight_ref.shape, 0)
    lane = lax.broadcasted_iota(jnp.int32, weight_ref.shape, 1)
    degree = (lax.axis_index(TAB) * weight_ref.shape[0] + cut) * weight_ref.shape[1] + lane
    degree_wide = degree.astype(jnp.float32)
    weight = jnp.sqrt(degree_wide * (degree_wide + 1.0))
    weight_ref[...] = jnp.where(degree >= order, weight, 0.0)


def longitude_rows(orders_ref, phase_ref):
    order_count = orders_ref.shape[0]
    points = phase_ref.shape[1]
    row = lax.broadcasted_iota(jnp.int32, (order_count, 128), 0)
    lane = lax.broadcasted_iota(jnp.int32, (order_count, 128), 1).astype(jnp.float32)
    order = jnp.zeros((order_count, 128), jnp.int32)
    for at in range(order_count):
        order = jnp.where(row == at, orders_ref[at], order)
    half_turn = (1 - 2 * (order & 1)).astype(jnp.float32).astype(jnp.bfloat16)
    order = order.astype(jnp.float32)
    first = order * lane
    quarter = points // 4
    for start in range(0, points // 2, 128):
        turn = first + order * float(start)
        quarters = jnp.floor(turn * (1.0 / quarter) + 0.5)
        x = (turn - quarters * float(quarter)) * (2.0 * math.pi / points)
        z = x * x
        sine = x * (1 + z * (-1 / 6 + z * (1 / 120 + z * (-1 / 5040 + z * (1 / 362880)))))
        cosine = 1 + z * (-1 / 2 + z * (1 / 24 + z * (-1 / 720 + z * (1 / 40320))))
        quarters = quarters.astype(jnp.int32)
        odd = (quarters & 1) == 1
        cos_row = jnp.where(odd, sine, cosine)
        sin_row = jnp.where(odd, cosine, sine)
        cos_row = jnp.where(((quarters + 1) & 2) == 0, 2.0, -2.0) * cos_row
        sin_row = jnp.where((quarters & 2) == 0, -2.0, 2.0) * sin_row
        cos_high, cos_low = halves(cos_row)
        sin_high, sin_low = halves(sin_row)
        for at, rows in enumerate([cos_high, sin_high, cos_low, sin_low, cos_high, sin_high]):
            place = slice(at * order_count, (at + 1) * order_count)
            phase_ref[place, start : start + 128] = rows
            start_2 = start + points // 2
            phase_ref[place, start_2 : start_2 + 128] = rows * half_turn


def near_place():
    return (1 - lax.axis_index("xl")) * 4 + lax.rem(lax.axis_index("zn") + 3, 4)


def own_order():
    return lax.axis_index("c") * len(NEAR_ORDER) + near_place()


def level_sums(poloidal, toroidal, orders):
    level_dev, order_count, _, degree_dev = poloidal.shape
    constants = level_constants(level_dev)
    return pl.pallas_call(
        level_kernel,
        out_shape=(
            pltpu.VMEM((order_count * 2 * degree_dev // 128, 3 * SHELLS, 128), jnp.bfloat16),
            pltpu.VMEM((order_count * 2 * degree_dev // 128, 3 * SHELLS, 128), jnp.float32),
            pltpu.VMEM((6 * order_count, NPHI), jnp.bfloat16),
            pltpu.VMEM((degree_dev // 128, 128), jnp.float32),
        ),
        in_specs=[pl.BlockSpec(memory_space=pltpu.HBM)] * 4,
        out_specs=[pl.BlockSpec(memory_space=pltpu.VMEM)] * 4,
        scratch_shapes=[
            pltpu.VMEM(constants.shape, jnp.float32),
            pltpu.VMEM(poloidal.shape, jnp.bfloat16),
            pltpu.VMEM(toroidal.shape, jnp.bfloat16),
            pltpu.SMEM(orders.shape, jnp.int32),
            pltpu.SemaphoreType.DMA((4,)),
        ],
        compiler_params=pltpu.CompilerParams(vmem_limit_bytes=57_000_000),
        name="level_sums",
    )(constants, poloidal, toroidal, orders)


def dot32(a, b):
    return jnp.dot(a, b, preferred_element_type=jnp.float32)


def projection_kernel(spectra_ref, table_ref, out_ref, held_ref):
    order_count = table_ref.shape[1]
    cuts = spectra_ref.shape[1] // 2

    def project(rows, table):
        return lax.dot_general(
            jnp.concatenate(rows, axis=0).astype(jnp.bfloat16),
            table,
            (((1,), (1,)), ((), ())),
            preferred_element_type=jnp.float32,
        )

    for order in range(order_count):
        blocks = [spectra_ref[order, at].astype(jnp.float32) for at in range(2 * cuts)]
        (q_re, q_im), (s_re, s_im), (t_re, t_im) = (
            [
                jnp.concatenate(
                    [
                        block[kind * SHELLS : (kind + 1) * SHELLS]
                        for block in blocks[part * cuts : (part + 1) * cuts]
                    ],
                    axis=1,
                )
                for part in range(2)
            ]
            for kind in range(3)
        )
        held_ref[0, order] = project([q_re, q_im], table_ref[0, order])
        pair = project([s_re, s_im, -t_re, -t_im], table_ref[1, order])
        pair += project([-t_im, t_re, -s_im, s_re], table_ref[2, order])
        held_ref[1, order] = pair[: 2 * SHELLS]
        held_ref[2, order] = pair[2 * SHELLS :]
    for shell in range(SHELLS):
        for part in range(2):
            rows = [held_ref[kind, :, part * SHELLS + shell, :] for kind in range(3)]
            out_ref[shell, part * order_count : (part + 1) * order_count, :] = jnp.concatenate(
                rows, axis=1
            ).astype(jnp.bfloat16)


def projection(spectra, tables):
    kinds, order_count, latitudes, _ = tables.shape
    return pl.pallas_call(
        projection_kernel,
        out_shape=pltpu.VMEM((SHELLS, 2 * order_count, kinds * latitudes), jnp.bfloat16),
        in_specs=[pl.BlockSpec(memory_space=pltpu.VMEM)] * 2,
        out_specs=pl.BlockSpec(memory_space=pltpu.VMEM),
        scratch_shapes=[pltpu.VMEM((kinds, order_count, 2 * SHELLS, latitudes), jnp.float32)],
        compiler_params=pltpu.CompilerParams(vmem_limit_bytes=16 << 20),
        name="projection",
    )(spectra, tables)


def synthesis_kernel(share_ref, phase_ref, out_hbm, chunk_ref, sems):
    chunks, _, width = chunk_ref.shape
    high, low = halves(jnp.sum(share_ref[...].astype(jnp.float32), axis=0))
    rows = jnp.concatenate([high, high, low], axis=0)
    copies = []
    for at in range(chunks):
        columns = slice(at * width, (at + 1) * width)
        values = lax.dot_general(
            rows,
            phase_ref[:, columns],
            (((0,), (0,)), ((), ())),
            preferred_element_type=jnp.float32,
        )
        chunk_ref[at] = values.astype(jnp.bfloat16)
        copies.append(
            pltpu.make_async_copy(chunk_ref.at[at], out_hbm.at[:, columns], sems.at[at])
        )
        copies[-1].start()
    for copy in copies:
        copy.wait()


def synthesis(shares, phases, chunks):
    rows, points = shares.shape[2], phases.shape[1]
    return pl.pallas_call(
        synthesis_kernel,
        out_shape=jax.ShapeDtypeStruct((rows, points), jnp.bfloat16),
        in_specs=[pl.BlockSpec(memory_space=pltpu.VMEM)] * 2,
        out_specs=pl.BlockSpec(memory_space=pltpu.HBM),
        scratch_shapes=[
            pltpu.VMEM((chunks, rows, points // chunks), jnp.bfloat16),
            pltpu.SemaphoreType.DMA((chunks,)),
        ],
        compiler_params=pltpu.CompilerParams(vmem_limit_bytes=16 << 20),
        name="synthesis",
    )(shares, phases)


def on_device(poloidal, toroidal, tables, orders):
    _, order_count, _, degree_dev = poloidal.shape
    half = order_count // 2
    blocks = half * 2 * degree_dev // 128
    near_count = lax.axis_size(NEAR)
    far_count = lax.axis_size("zf")
    core = lax.axis_index("c")
    partial, own, phases, weight = level_sums(poloidal, toroidal, orders)
    pair = lax.all_gather(partial, "c", axis=0)
    partner = lax.dynamic_slice(
        pair, (1 - core, core * blocks, 0, 0), (1, blocks) + pair.shape[2:]
    )
    own = lax.dynamic_slice_in_dim(own, core * blocks, blocks, 0)
    partial = (own + partner[0].astype(jnp.float32)).astype(jnp.bfloat16)
    shares = lax.all_to_all(partial, NEAR, 0, 0, axis_index_groups=[NEAR_ORDER], tiled=True)
    shares = shares.reshape(near_count, -1, 3 * SHELLS, 128).astype(jnp.float32)
    near_sum = lax.optimization_barrier(jnp.sum(shares, axis=0))
    copies = jnp.broadcast_to(near_sum.astype(jnp.bfloat16), (far_count,) + near_sum.shape)
    shares = lax.all_to_all(copies, "zf", 0, 0, axis_index_groups=[FAR_ORDER], tiled=True)
    radial = jnp.sum(shares.astype(jnp.float32), axis=0)
    radial = radial.reshape(2, degree_dev // 128, 3, SHELLS, 128)
    weight = weight.reshape(1, degree_dev // 128, 1, 128)
    spheroidal = radial[:, :, 0] / shell_radius()[:, None]
    spectra = jnp.stack(
        [
            weight * spheroidal,
            weight * (spheroidal + radial[:, :, 1]),
            weight * radial[:, :, 2],
        ],
        axis=2,
    ).astype(jnp.bfloat16)
    spectra = jnp.broadcast_to(
        spectra.reshape(1, -1, 3 * SHELLS, 128), (near_count, blocks // near_count, 3 * SHELLS, 128)
    )
    spectra = lax.all_to_all(spectra, NEAR, 0, 0, axis_index_groups=[NEAR_ORDER], tiled=True)
    spectra = lax.all_gather(spectra, "c", axis=0, tiled=True)
    fourier = projection(spectra.reshape(order_count, -1, 3 * SHELLS, 128), tables)
    fourier = lax.all_to_all(fourier, TAB, 0, 0, axis_index_groups=[TAB_ORDER], tiled=True)
    return synthesis(fourier, phases, 4).reshape(3, 1, -1, NPHI)


def solution(mesh):
    fine = Mesh(mesh.devices.reshape(2, 4, 2, 4, 4, 2), TAB + RAD)
    placed = (
        P(RAD, None, None, TAB),
        P(RAD, None, None, TAB),
        P(None, None, RAD, TAB),
        P(),
    )
    return jax.shard_map(
        on_device,
        mesh=fine,
        in_specs=placed,
        out_specs=P(None, TAB, RAD, None),
        check_vma=False,
    )
```

```python
import math

import jax
import jax.numpy as jnp
import numpy as np
from jax import lax
from jax.experimental import pallas as pl
from jax.experimental.pallas import tpu as pltpu
from jax.sharding import Mesh, PartitionSpec as P

NPHI = 6144
SHELLS = 8
RAD = ("xl", "zf", "zn", "c")
NEAR = ("xl", "zn")
NEAR_ORDER = (5, 6, 7, 4, 1, 2, 3, 0)
FAR_ORDER = (2, 3, 0, 1)
TAB_ORDER = (6, 2, 7, 3, 5, 1, 4, 0)
TAB = ("xh", "y")


def shell_radius():
    angle = math.pi / (2 * SHELLS) * (2 * np.array(TAB_ORDER) + 1)
    return (1.04 + 0.5 * np.cos(angle)).astype(np.float32)


def level_constants(level_dev):
    row = np.arange(2 * 3 * SHELLS)[:, None]
    col = np.arange(4 * level_dev * 2)[None, :]
    kind = row % (3 * SHELLS) // SHELLS
    odd = 2 * np.array(TAB_ORDER)[row % SHELLS] + 1
    source = col // (2 * level_dev)
    used = (row // (3 * SHELLS) == col % 2) & ((kind < 2) == (source < 2))
    step_angle = math.pi / (2 * SHELLS)
    planes = []
    for parity in range(4 * SHELLS // level_dev):
        level = parity * level_dev + col % (2 * level_dev) // 2
        angle = step_angle * (level * odd % (4 * SHELLS))
        value = np.where(used & (kind != 1), np.cos(angle), 0.0)
        slope = np.where(used & (kind == 1), 2.0 * np.sin(angle) / np.sin(step_angle * odd), 0.0)
        planes.append(np.stack([value, slope]))
    return np.stack(planes).astype(np.float32)


def level_kernel(
    constant_hbm, pol_hbm, tor_hbm, orders_hbm, out_ref, own_ref, phase_ref, weight_ref,
    constant_ref, pol_ref, tor_ref, orders_ref, sems,
):
    loads = [
        pltpu.make_async_copy(source, target, sems.at[at])
        for at, (source, target) in enumerate(
            [
                (orders_hbm, orders_ref),
                (constant_hbm, constant_ref),
                (pol_hbm, pol_ref),
                (tor_hbm, tor_ref),
            ]
        )
    ]
    for at, load in enumerate(loads):
        load.start(priority=at % 2)
    loads[0].wait()
    weight_rows(orders_ref, weight_ref)
    longitude_rows(orders_ref, phase_ref)
    for load in loads[1:]:
        load.wait()

    level_dev, order_count, _, degree_dev = pol_ref.shape
    rows = out_ref.shape[1]
    run = lax.axis_index(RAD)
    plane = lax.rem(run, constant_ref.shape[0])
    col = lax.broadcasted_iota(jnp.int32, constant_ref.shape[2:], 1)
    level = (run * level_dev + col % (2 * level_dev) // 2).astype(jnp.float32)
    entry = constant_ref[plane, 0] + level * constant_ref[plane, 1]
    high, low = halves(entry)
    matrix = jnp.where(col // (2 * level_dev) % 2 == 0, high, low)
    for order in range(order_count):
        pol = pol_ref[:, order].reshape(2 * level_dev, degree_dev)
        tor = tor_ref[:, order].reshape(2 * level_dev, degree_dev)
        sums = dot32(matrix, jnp.concatenate([pol, pol, tor, tor], axis=0))
        for part in range(2):
            for cut in range(degree_dev // 128):
                block = sums[part * rows : (part + 1) * rows, cut * 128 : (cut + 1) * 128]
                at = (order * 2 + part) * (degree_dev // 128) + cut
                out_ref[at] = block.astype(jnp.bfloat16)
                own_ref[at] = block


def halves(x):
    high = x.astype(jnp.bfloat16)
    return high, (x - high.astype(jnp.float32)).astype(jnp.bfloat16)


def weight_rows(orders_ref, weight_ref):
    order = orders_ref[own_order()]
    cut = lax.broadcasted_iota(jnp.int32, weight_ref.shape, 0)
    lane = lax.broadcasted_iota(jnp.int32, weight_ref.shape, 1)
    degree = (lax.axis_index(TAB) * weight_ref.shape[0] + cut) * weight_ref.shape[1] + lane
    degree_wide = degree.astype(jnp.float32)
    weight = jnp.sqrt(degree_wide * (degree_wide + 1.0))
    weight_ref[...] = jnp.where(degree >= order, weight, 0.0)


def longitude_rows(orders_ref, phase_ref):
    order_count = orders_ref.shape[0]
    points = phase_ref.shape[1]
    row = lax.broadcasted_iota(jnp.int32, (order_count, 128), 0)
    lane = lax.broadcasted_iota(jnp.int32, (order_count, 128), 1).astype(jnp.float32)
    order = jnp.zeros((order_count, 128), jnp.int32)
    for at in range(order_count):
        order = jnp.where(row == at, orders_ref[at], order)
    half_turn = (1 - 2 * (order & 1)).astype(jnp.float32).astype(jnp.bfloat16)
    order = order.astype(jnp.float32)
    first = order * lane
    quarter = points // 4
    for start in range(0, points // 2, 128):
        turn = first + order * float(start)
        quarters = jnp.floor(turn * (1.0 / quarter) + 0.5)
        x = (turn - quarters * float(quarter)) * (2.0 * math.pi / points)
        z = x * x
        sine = x * (1 + z * (-1 / 6 + z * (1 / 120 + z * (-1 / 5040 + z * (1 / 362880)))))
        cosine = 1 + z * (-1 / 2 + z * (1 / 24 + z * (-1 / 720 + z * (1 / 40320))))
        quarters = quarters.astype(jnp.int32)
        odd = (quarters & 1) == 1
        cos_row = jnp.where(odd, sine, cosine)
        sin_row = jnp.where(odd, cosine, sine)
        cos_row = jnp.where(((quarters + 1) & 2) == 0, 2.0, -2.0) * cos_row
        sin_row = jnp.where((quarters & 2) == 0, -2.0, 2.0) * sin_row
        cos_high, cos_low = halves(cos_row)
        sin_high, sin_low = halves(sin_row)
        for at, rows in enumerate([cos_high, sin_high, cos_low, sin_low, cos_high, sin_high]):
            place = slice(at * order_count, (at + 1) * order_count)
            phase_ref[place, start : start + 128] = rows
            start_2 = start + points // 2
            phase_ref[place, start_2 : start_2 + 128] = rows * half_turn


def near_place():
    return (1 - lax.axis_index("xl")) * 4 + lax.rem(lax.axis_index("zn") + 3, 4)


def own_order():
    return lax.axis_index("c") * len(NEAR_ORDER) + near_place()


def level_sums(poloidal, toroidal, orders):
    level_dev, order_count, _, degree_dev = poloidal.shape
    constants = level_constants(level_dev)
    return pl.pallas_call(
        level_kernel,
        out_shape=(
            pltpu.VMEM((order_count * 2 * degree_dev // 128, 3 * SHELLS, 128), jnp.bfloat16),
            pltpu.VMEM((order_count * 2 * degree_dev // 128, 3 * SHELLS, 128), jnp.float32),
            pltpu.VMEM((6 * order_count, NPHI), jnp.bfloat16),
            pltpu.VMEM((degree_dev // 128, 128), jnp.float32),
        ),
        in_specs=[pl.BlockSpec(memory_space=pltpu.HBM)] * 4,
        out_specs=[pl.BlockSpec(memory_space=pltpu.VMEM)] * 4,
        scratch_shapes=[
            pltpu.VMEM(constants.shape, jnp.float32),
            pltpu.VMEM(poloidal.shape, jnp.bfloat16),
            pltpu.VMEM(toroidal.shape, jnp.bfloat16),
            pltpu.SMEM(orders.shape, jnp.int32),
            pltpu.SemaphoreType.DMA((4,)),
        ],
        compiler_params=pltpu.CompilerParams(vmem_limit_bytes=57_000_000),
        name="level_sums",
    )(constants, poloidal, toroidal, orders)


def dot32(a, b):
    return jnp.dot(a, b, preferred_element_type=jnp.float32)


def projection_kernel(spectra_ref, table_ref, out_ref, held_ref):
    order_count = table_ref.shape[1]
    cuts = spectra_ref.shape[1] // 2

    def project(rows, table):
        return lax.dot_general(
            jnp.concatenate(rows, axis=0).astype(jnp.bfloat16),
            table,
            (((1,), (1,)), ((), ())),
            preferred_element_type=jnp.float32,
        )

    for order in range(order_count):
        blocks = [spectra_ref[order, at].astype(jnp.float32) for at in range(2 * cuts)]
        (q_re, q_im), (s_re, s_im), (t_re, t_im) = (
            [
                jnp.concatenate(
                    [
                        block[kind * SHELLS : (kind + 1) * SHELLS]
                        for block in blocks[part * cuts : (part + 1) * cuts]
                    ],
                    axis=1,
                )
                for part in range(2)
            ]
            for kind in range(3)
        )
        held_ref[0, order] = project([q_re, q_im], table_ref[0, order])
        pair = project([s_re, s_im, -t_re, -t_im], table_ref[1, order])
        pair += project([-t_im, t_re, -s_im, s_re], table_ref[2, order])
        held_ref[1, order] = pair[: 2 * SHELLS]
        held_ref[2, order] = pair[2 * SHELLS :]
    for shell in range(SHELLS):
        for part in range(2):
            rows = [held_ref[kind, :, part * SHELLS + shell, :] for kind in range(3)]
            out_ref[shell, part * order_count : (part + 1) * order_count, :] = jnp.concatenate(
                rows, axis=1
            ).astype(jnp.bfloat16)


def projection(spectra, tables):
    kinds, order_count, latitudes, _ = tables.shape
    return pl.pallas_call(
        projection_kernel,
        out_shape=pltpu.VMEM((SHELLS, 2 * order_count, kinds * latitudes), jnp.bfloat16),
        in_specs=[pl.BlockSpec(memory_space=pltpu.VMEM)] * 2,
        out_specs=pl.BlockSpec(memory_space=pltpu.VMEM),
        scratch_shapes=[pltpu.VMEM((kinds, order_count, 2 * SHELLS, latitudes), jnp.float32)],
        compiler_params=pltpu.CompilerParams(vmem_limit_bytes=16 << 20),
        name="projection",
    )(spectra, tables)


def synthesis_kernel(share_ref, phase_ref, out_hbm, chunk_ref, sems):
    chunks, _, width = chunk_ref.shape
    high, low = halves(jnp.sum(share_ref[...].astype(jnp.float32), axis=0))
    rows = jnp.concatenate([high, high, low], axis=0)
    copies = []
    for at in range(chunks):
        columns = slice(at * width, (at + 1) * width)
        values = lax.dot_general(
            rows,
            phase_ref[:, columns],
            (((0,), (0,)), ((), ())),
            preferred_element_type=jnp.float32,
        )
        chunk_ref[at] = values.astype(jnp.bfloat16)
        copies.append(
            pltpu.make_async_copy(chunk_ref.at[at], out_hbm.at[:, columns], sems.at[at])
        )
        copies[-1].start(priority=at % 2)
    for copy in copies:
        copy.wait()


def synthesis(shares, phases, chunks):
    rows, points = shares.shape[2], phases.shape[1]
    return pl.pallas_call(
        synthesis_kernel,
        out_shape=jax.ShapeDtypeStruct((rows, points), jnp.bfloat16),
        in_specs=[pl.BlockSpec(memory_space=pltpu.VMEM)] * 2,
        out_specs=pl.BlockSpec(memory_space=pltpu.HBM),
        scratch_shapes=[
            pltpu.VMEM((chunks, rows, points // chunks), jnp.bfloat16),
            pltpu.SemaphoreType.DMA((chunks,)),
        ],
        compiler_params=pltpu.CompilerParams(vmem_limit_bytes=16 << 20),
        name="synthesis",
    )(shares, phases)


def on_device(poloidal, toroidal, tables, orders):
    _, order_count, _, degree_dev = poloidal.shape
    half = order_count // 2
    blocks = half * 2 * degree_dev // 128
    near_count = lax.axis_size(NEAR)
    far_count = lax.axis_size("zf")
    core = lax.axis_index("c")
    partial, own, phases, weight = level_sums(poloidal, toroidal, orders)
    pair = lax.all_gather(partial, "c", axis=0)
    partner = lax.dynamic_slice(
        pair, (1 - core, core * blocks, 0, 0), (1, blocks) + pair.shape[2:]
    )
    own = lax.dynamic_slice_in_dim(own, core * blocks, blocks, 0)
    partial = (own + partner[0].astype(jnp.float32)).astype(jnp.bfloat16)
    shares = lax.all_to_all(partial, NEAR, 0, 0, axis_index_groups=[NEAR_ORDER], tiled=True)
    shares = shares.reshape(near_count, -1, 3 * SHELLS, 128).astype(jnp.float32)
    near_sum = lax.optimization_barrier(jnp.sum(shares, axis=0))
    copies = jnp.broadcast_to(near_sum.astype(jnp.bfloat16), (far_count,) + near_sum.shape)
    shares = lax.all_to_all(copies, "zf", 0, 0, axis_index_groups=[FAR_ORDER], tiled=True)
    radial = jnp.sum(shares.astype(jnp.float32), axis=0)
    radial = radial.reshape(2, degree_dev // 128, 3, SHELLS, 128)
    weight = weight.reshape(1, degree_dev // 128, 1, 128)
    spheroidal = radial[:, :, 0] / shell_radius()[:, None]
    spectra = jnp.stack(
        [
            weight * spheroidal,
            weight * (spheroidal + radial[:, :, 1]),
            weight * radial[:, :, 2],
        ],
        axis=2,
    ).astype(jnp.bfloat16)
    spectra = jnp.broadcast_to(
        spectra.reshape(1, -1, 3 * SHELLS, 128), (near_count, blocks // near_count, 3 * SHELLS, 128)
    )
    spectra = lax.all_to_all(spectra, NEAR, 0, 0, axis_index_groups=[NEAR_ORDER], tiled=True)
    spectra = lax.all_gather(spectra, "c", axis=0, tiled=True)
    fourier = projection(spectra.reshape(order_count, -1, 3 * SHELLS, 128), tables)
    fourier = lax.all_to_all(fourier, TAB, 0, 0, axis_index_groups=[TAB_ORDER], tiled=True)
    return synthesis(fourier, phases, 4).reshape(3, 1, -1, NPHI)


def solution(mesh):
    fine = Mesh(mesh.devices.reshape(2, 4, 2, 4, 4, 2), TAB + RAD)
    placed = (
        P(RAD, None, None, TAB),
        P(RAD, None, None, TAB),
        P(None, None, RAD, TAB),
        P(),
    )
    return jax.shard_map(
        on_device,
        mesh=fine,
        in_specs=placed,
        out_specs=P(None, TAB, RAD, None),
        check_vma=False,
    )
```
